32 devices in a mesh: pos: 16 (over z, x, core), off: 2 (over y).
Axes of the slice: x: 2, y: 2, z: 4, core: 2. Of those that a mesh axis runs over, the one named last changes fastest.
Arguments:
- bin_embed: bfloat16 [1024, 128], P('pos'), may hold values from -6 to 6
- block_slot: int32 [16], replicated, may hold values from 0 to 15, each once
- proj_weight: bfloat16 [128, 64], replicated, may hold values from -0.5 to 0.5
- proj_bias: float32 [64], replicated, may hold values from -3 to 3
- conv_weight: bfloat16 [4, 576, 64], replicated, may hold values from -0.25 to 0.25
- conv_bias: float32 [4, 64], replicated, may hold values from -2 to 2
Outputs:
- contact: bfloat16 [16, 2, 64, 4096], P('pos', 'off')
The draws below stay inside these ranges and needn't reach their ends.
Inputs may be any that keep to these rules, and one draw needn't show every extreme that they name: block_slot names every number of 0 to 15 once; bin block b's embeddings are rows block_slot[b] * 64 to block_slot[b] * 64 + 63 of bin_embed.
All inputs are finite; a program needn't handle non-finite values.
Results may differ from the reference program's by a relative error of at most 0.015.
Values may be sent and summed in bfloat16 or wider, within the bound.
No kernel may reach another device: no remote copies, remote signals or barrier semaphores. Data moves between devices by JAX's collectives and lax.ppermute only.
A program may use at most 64 MiB of HBM per device.

```python
import jax
import jax.numpy as jnp
import numpy as np
from jax import lax

TILE = 64
CH = 64
EMB = 128
LAYERS = 4
NPOS = 16
NOFF = 2


def shard_levels(rng, dims, shards, low, high):
    def one(dim, shards_of):
        draws = jax.random.uniform(jax.random.fold_in(jax.random.fold_in(rng, 6), dim), (shards_of,), jnp.float32, low / len(shards), high / len(shards))
        return jnp.repeat(jnp.exp(draws), dims[dim] // shards_of).reshape((-1,) + (1,) * (len(dims) - dim - 1))

    factor_of = one(*shards[0])
    for cut in shards[1:]:
        factor_of = factor_of * one(*cut)
    return factor_of


def gaussian(key, dims, width, reach, split=(), kind=jnp.bfloat16):
    drawn = jax.random.normal(key, dims, jnp.float32) * width
    if len(split) > 0:
        drawn = shard_levels(key, dims, split, -0.22, 0.18) * drawn
    return jnp.clip(drawn, min=-reach, max=reach).astype(kind)


def setup_inputs(seed: int = 0) -> dict:
    seeds = jax.random.split(jax.random.key(seed), 7)
    return {
        "bin_embed": gaussian(seeds[0], (NPOS * TILE, EMB), 1.0, 6.0, ((0, 16),)),
        "block_slot": jax.random.permutation(seeds[1], NPOS).astype(jnp.int32),
        "proj_weight": gaussian(seeds[2], (EMB, CH), EMB ** -0.5, 0.5),
        "proj_bias": gaussian(seeds[3], (CH,), 0.5, 3.0, (), jnp.float32),
        "conv_weight": gaussian(seeds[4], (LAYERS, 9 * CH, CH), (9 * CH) ** -0.5, 0.25),
        "conv_bias": gaussian(seeds[5], (LAYERS, CH), 0.3, 2.0, (), jnp.float32),
    }


def flip_tiles(tiles):
    return jnp.swapaxes(tiles, -3, -2)


def reference(bin_embed, block_slot, proj_weight, proj_bias, conv_weight, conv_bias):
    projected = jnp.dot(bin_embed, proj_weight, preferred_element_type=jnp.float32).astype(jnp.bfloat16)
    projected = projected.reshape(NPOS, TILE, CH)[block_slot]
    col_index = (jnp.arange(NPOS)[:, None] + jnp.arange(NOFF)[None, :]) % NPOS
    col_bins = projected[col_index]
    pair_sum = projected[:, None, :, None, :].astype(jnp.float32) + col_bins[:, :, None, :, :].astype(jnp.float32) + proj_bias
    current = pair_sum.astype(jnp.bfloat16)
    for layer_index in range(LAYERS):
        dilation = 2 ** layer_index
        hidden = jax.nn.gelu(current.astype(jnp.float32)).astype(jnp.bfloat16)
        mirrors = []
        for mirror_band in (2, 1):
            if mirror_band < NOFF:
                mirrors.append(jnp.roll(flip_tiles(hidden[:, mirror_band]), mirror_band, axis=0)[:, None])
            else:
                mirrors.append(jnp.zeros_like(hidden[:, :1]))
        beyond = jnp.zeros_like(hidden[:, :1])
        extended = jnp.concatenate(mirrors + [hidden, beyond, beyond], axis=1)
        weights = conv_weight[layer_index].astype(jnp.float32)
        layer_bias = conv_bias[layer_index]

        def one_row(inputs, extended=extended, weights=weights, layer_bias=layer_bias, dilation=dilation):
            position, tile_row = inputs
            rows_out = []
            for shift_row in (-1, 0, 1):
                source = extended[(position + shift_row) % NPOS]
                pieces = [source[np.arange(NOFF) + shift_col - shift_row + 2] for shift_col in (-1, 0, 1)]
                rows_out.append(jnp.concatenate(pieces, axis=2))
            padded = jnp.concatenate(rows_out, axis=1)
            padded = padded[:, TILE - dilation:2 * TILE + dilation, TILE - dilation:2 * TILE + dilation].astype(jnp.float32)
            summed = jnp.zeros((NOFF, TILE, TILE, CH), jnp.float32)
            for row_tap in range(3):
                for col_tap in range(3):
                    tap_index = 3 * row_tap + col_tap
                    window = padded[:, row_tap * dilation:row_tap * dilation + TILE, col_tap * dilation:col_tap * dilation + TILE]
                    summed = summed + jnp.einsum("orcd,de->orce", window, weights[tap_index * CH:(tap_index + 1) * CH])
            return (tile_row.astype(jnp.float32) + summed + layer_bias).astype(jnp.bfloat16)

        current = lax.map(one_row, (jnp.arange(NPOS, dtype=jnp.int32), current))
    return current.reshape(NPOS, NOFF, TILE, TILE * CH)
```

```python
import functools

import jax
import jax.numpy as jnp
from jax import lax
from jax.experimental import pallas as pl
from jax.experimental.pallas import tpu as pltpu
from jax.sharding import PartitionSpec as P

GROUP = 4
BASE = 8


def gelu(x):
    u = x * (0.7978845608028654 + 0.035677408136300125 * (x * x))
    half = 0.5 * x
    return half + half * jnp.tanh(u)


def place(col, halo, dil):
    u = col + halo
    within = u % (2 * dil)
    return (u // (2 * dil)) * dil + within % dil, within // dil


def columns(group, halo, dil):
    first = (group // dil) * 2 * dil + group % dil - halo
    return first, first + dil


def weights_kernel(layers, ch, cw_ref, t_ref):
    zero = jnp.zeros((ch, ch), t_ref.dtype)
    for l in range(layers):
        for i in range(3):
            taps = [cw_ref[l, (3 * i + j) * ch : (3 * i + j + 1) * ch, :] for j in range(3)]
            for a in range(6):
                row = [taps[a - b] if 0 <= a - b <= 2 else zero for b in (0, 2, 1, 3)]
                t_ref[l, (6 * i + a) * ch : (6 * i + a + 1) * ch, :] = jnp.concatenate(row, axis=1)


def tile_kernel(
    dims, slot_ref, emb_ref, pw_ref, pb_ref, t_ref, cb_ref, out_ref, x_ref, g_ref, h_ref, z_ref, bins_ref
):
    layers, tile, ch, npos, noff, order = dims
    wide = 2 * ch
    edge = 16
    rows = tile + 2 * edge
    halos = [2**layers - 2**l for l in range(layers + 1)]
    me, off = lax.axis_index("pos"), lax.axis_index("off")
    low = lax.broadcasted_iota(jnp.int32, (1, wide), 1) < ch

    def pick(lo, hi):
        return jnp.where(low, lo, hi)

    def both(value, half):
        turned = pltpu.roll(value, ch, 1)
        return pick(turned, value) if half else pick(value, turned)

    def block(b):
        away = jnp.bitwise_xor(slot_ref[lax.rem(b + npos, npos)], me)
        index = 0
        for place_in, bit in enumerate(order):
            index += jnp.bitwise_and(lax.shift_right_logical(away, bit), 1) << place_in
        return index

    pw = pw_ref[...]
    pw = jnp.concatenate([pw, pw], axis=1)

    def bins(b):
        first, here, last = (emb_ref[block(b + k)] for k in (-1, 0, 1))
        picked = jnp.concatenate([first[tile - edge :], here, last[:edge]], axis=0)
        return jnp.dot(picked, pw, preferred_element_type=jnp.float32).astype(jnp.bfloat16).astype(jnp.float32)

    row_bins = bins(me) + pb_ref[...]
    bins_ref[...] = bins(me + off)
    pairs = (tile + 2 * halos[0]) // 2
    first = edge - halos[0]
    col_bins = pick(
        bins_ref[pl.ds(first, pairs, stride=2), :], bins_ref[pl.ds(first + 1, pairs, stride=2), :]
    )

    def keep(a, b):
        return (jnp.abs(off + b - a) < noff).astype(jnp.float32)

    keeps = {(a, b): keep(a, b) for a in (-1, 0, 1) for b in (-1, 0, 1)}

    def band(col):
        return -1 if col < 0 else 1 if col >= tile else 0

    def activate(l, group, x, start):
        lo, hi = (band(c) for c in columns(group, halos[l], 2**l))
        size = x.shape[0]
        for a, begin, end in ((-1, 0, edge), (0, edge, edge + tile), (1, edge + tile, rows)):
            begin, end = max(begin, start), min(end, start + size)
            if begin >= end:
                continue
            g = gelu(x[begin - start : end - start])
            if (a, lo, hi) != (0, 0, 0):
                g = g * pick(keeps[a, lo], keeps[a, hi])
            g_ref[group, BASE + begin : BASE + end, :] = g

    def mirror(l):
        halo, dil = halos[l], 2**l
        groups = (tile + 2 * halo) // 2
        deep = -(-halo // 8) * 8
        top, mid, bot = BASE, BASE + edge, BASE + edge + tile

        def write_bottom(group, c1, c2, limit):
            if c1 >= limit:
                return
            lo = z_ref[(c1 + edge) * edge : (c1 + edge) * edge + deep, :]
            if c2 < limit:
                hi = z_ref[(c2 + edge) * edge : (c2 + edge) * edge + deep, :]
            else:
                hi = g_ref[group, bot : bot + deep, :]
            g_ref[group, bot : bot + deep, :] = pick(lo, hi)

        @pl.when(off == 0)
        def _():
            for k in range(halo):
                group, half = place(tile + k, halo, dil)
                z_ref[pl.ds(k, edge + tile, stride=edge), :] = both(g_ref[group, top:bot, :], half)
            for group in range(groups):
                write_bottom(group, *columns(group, halo, dil), tile)
            for r in range(tile):
                group, half = place(r, halo, dil)
                z_ref[pl.ds(r, edge, stride=tile), :] = both(g_ref[group, top:mid, :], half)
            for group in range(groups):
                c1, c2 = columns(group, halo, dil)
                if c1 < 0:
                    lo = z_ref[(c1 + edge) * tile : (c1 + edge + 1) * tile, :]
                    if c2 < 0:
                        hi = z_ref[(c2 + edge) * tile : (c2 + edge + 1) * tile, :]
                    else:
                        hi = g_ref[group, mid:bot, :]
                    g_ref[group, mid:bot, :] = pick(lo, hi)

        @pl.when(off == 1)
        def _():
            for k in range(halo):
                group, half = place(k, halo, dil)
                z_ref[pl.ds(k, edge, stride=edge), :] = both(g_ref[group, bot - edge : bot, :], half)
            for group in range(groups):
                write_bottom(group, *columns(group, halo, dil), 0)

    for group in range(pairs):
        x = row_bins + col_bins[group : group + 1]
        x_ref[0, group, :, :] = x
        activate(0, group, x, 0)

    for l in range(layers):
        dil = 2**l
        start = (edge - halos[l + 1]) // 8 * 8
        size = rows - 2 * start
        groups = (tile + 2 * halos[l]) // 2
        if l:
            mirror(l)
        for group in range(groups):
            for i in range(3):
                begin = BASE + start + (i - 1) * dil
                h_ref[i, group, 0:size, :] = g_ref[group, begin : begin + size, :].astype(jnp.bfloat16)
        blocks = [(j, e) for j in range((tile + 2 * halos[l + 1]) // (4 * dil)) for e in range(dil)]
        bias = cb_ref[l : l + 1, :]
        now, later = l % 2, (l + 1) % 2
        done = {}
        for at in range(0, len(blocks), GROUP):
            some = blocks[at : at + GROUP]
            lhs = jnp.concatenate(
                [
                    jnp.concatenate(
                        [h_ref[i, (2 * j + s) * dil + e, 0:size, :] for i in range(3) for s in range(3)], axis=1
                    )
                    for j, e in some
                ],
                axis=0,
            )
            acc = jnp.dot(lhs, t_ref[l], preferred_element_type=jnp.float32)
            for n, (j, e) in enumerate(some):
                old = [x_ref[now, (2 * j + s) * dil + e, start : start + size, :] for s in range(3)]
                carried = (
                    pick(pltpu.roll(old[0], ch, 1), old[1]),
                    pick(old[1], pltpu.roll(old[2], ch, 1)),
                )
                for s in range(2):
                    x = acc[n * size : (n + 1) * size, s * wide : (s + 1) * wide] + carried[s] + bias
                    group = j * 2 * dil + e + s * dil
                    if l + 1 < layers:
                        x_ref[later, group, start : start + size, :] = x
                        activate(l + 1, group, x, start)
                    else:
                        x_ref[later, group, start : start + size, :] = x
    final = layers % 2
    stretch = 2**layers
    for j in range(tile // (2 * stretch)):
        for e in range(0, stretch, 2):
            even, odd = (
                x_ref[final, j * stretch + e + s, edge : edge + tile, :] for s in range(2)
            )
            col = 2 * stretch * j + e
            out_ref[:, col * ch : (col + 2) * ch] = pick(even, pltpu.roll(odd, ch, 1)).astype(out_ref.dtype)
            col += stretch
            out_ref[:, col * ch : (col + 2) * ch] = pick(pltpu.roll(even, ch, 1), odd).astype(out_ref.dtype)


def on_device(bin_embed, block_slot, proj_weight, proj_bias, conv_weight, conv_bias):
    npos, noff = lax.axis_size("pos"), lax.axis_size("off")
    tile, emb = bin_embed.shape
    layers, taps, ch = conv_weight.shape
    bits = npos.bit_length() - 1
    order = tuple(reversed(range(bits)))
    table = bin_embed[None]
    for bit in order:
        there = lax.ppermute(table, "pos", [(i, i ^ (1 << bit)) for i in range(npos)])
        table = jnp.concatenate([table, there], axis=0)
    vmem = pl.BlockSpec(memory_space=pltpu.VMEM)
    toeplitz = pl.pallas_call(
        functools.partial(weights_kernel, layers, ch),
        out_shape=jax.ShapeDtypeStruct((layers, 2 * taps, 4 * ch), conv_weight.dtype),
        in_specs=[vmem],
        out_specs=vmem,
        cost_estimate=pl.CostEstimate(flops=2000000, bytes_accessed=4000000, transcendentals=0),
    )(conv_weight)
    wide = 2 * ch
    groups = tile // 2 + 2**layers - 1
    high = tile + 32
    out = pl.pallas_call(
        functools.partial(tile_kernel, (layers, tile, ch, npos, noff, order)),
        out_shape=jax.ShapeDtypeStruct((tile, tile * ch), jnp.bfloat16),
        in_specs=[pl.BlockSpec(memory_space=pltpu.SMEM)] + [vmem] * 5,
        out_specs=vmem,
        scratch_shapes=[
            pltpu.VMEM((2, groups, high, wide), jnp.float32),
            pltpu.VMEM((groups, high + 2 * BASE, wide), jnp.float32),
            pltpu.VMEM((3, groups, high, wide), jnp.bfloat16),
            pltpu.VMEM((16 * (tile + 16), wide), jnp.float32),
            pltpu.VMEM((high, wide), jnp.float32),
        ],
        compiler_params=pltpu.CompilerParams(vmem_limit_bytes=48 * 1024 * 1024),
        cost_estimate=pl.CostEstimate(flops=8000000000, bytes_accessed=4000000, transcendentals=2000000),
    )(
        block_slot,
        table,
        proj_weight,
        jnp.concatenate([proj_bias, proj_bias])[None],
        toeplitz,
        jnp.concatenate([conv_bias, conv_bias], axis=1),
    )
    return out.reshape(1, 1, tile, tile * ch)


def solution(mesh):
    placed = (P("pos", None), P(), P(), P(), P(), P())
    return jax.shard_map(
        on_device,
        mesh=mesh,
        in_specs=placed,
        out_specs=P("pos", "off", None, None),
        check_vma=False,
    )
```

```python
import functools

import jax
import jax.numpy as jnp
from jax import lax
from jax.experimental import pallas as pl
from jax.experimental.pallas import tpu as pltpu
from jax.sharding import PartitionSpec as P

GROUP = 4
BASE = 8


def gelu(x):
    u = x * (0.7978845608028654 + 0.035677408136300125 * (x * x))
    half = 0.5 * x
    return half + half * jnp.tanh(u)


def place(col, halo, dil):
    u = col + halo
    within = u % (2 * dil)
    return (u // (2 * dil)) * dil + within % dil, within // dil


def columns(group, halo, dil):
    first = (group // dil) * 2 * dil + group % dil - halo
    return first, first + dil


def weights_kernel(ch, cw_ref, t_ref):
    taps = jnp.transpose(cw_ref[...].astype(jnp.float32)).astype(t_ref.dtype)
    zero = jnp.zeros((ch, ch), t_ref.dtype)
    for i in range(3):
        for a in range(6):
            row = [
                taps[(3 * i + a - b) * ch : (3 * i + a - b + 1) * ch] if 0 <= a - b <= 2 else zero
                for b in (0, 2, 1, 3)
            ]
            t_ref[(6 * i + a) * ch : (6 * i + a + 1) * ch, :] = jnp.concatenate(row, axis=1)


def tile_kernel(
    dims, slot_ref, emb_ref, pw_ref, pb_ref, cb_ref, *refs
):
    t_refs, (out_ref, x_ref, g_ref, h_ref, z_ref, bins_ref) = refs[: dims[0]], refs[dims[0] :]
    layers, tile, ch, npos, noff, order = dims
    wide = 2 * ch
    edge = 16
    rows = tile + 2 * edge
    halos = [2**layers - 2**l for l in range(layers + 1)]
    me, off = lax.axis_index("pos"), lax.axis_index("off")
    low = lax.broadcasted_iota(jnp.int32, (1, wide), 1) < ch

    def pick(lo, hi):
        return jnp.where(low, lo, hi)

    def both(value, half):
        turned = pltpu.roll(value, ch, 1)
        return pick(turned, value) if half else pick(value, turned)

    def block(b):
        away = jnp.bitwise_xor(slot_ref[lax.rem(b + npos, npos)], me)
        index = 0
        for place_in, bit in enumerate(order):
            index += jnp.bitwise_and(lax.shift_right_logical(away, bit), 1) << place_in
        return index

    pw = pw_ref[...]

    def bins(b):
        first, here, last = (emb_ref[block(b + k)] for k in (-1, 0, 1))
        picked = jnp.concatenate([first[tile - edge :], here, last[:edge]], axis=0)
        made = lax.dot_general(picked, pw, (((1,), (1,)), ((), ())), preferred_element_type=jnp.float32)
        return made.astype(jnp.bfloat16).astype(jnp.float32)

    row_bins = bins(me) + pb_ref[...]
    bins_ref[...] = bins(me + off)
    pairs = (tile + 2 * halos[0]) // 2
    first = edge - halos[0]
    col_bins = pick(
        bins_ref[pl.ds(first, pairs, stride=2), :], bins_ref[pl.ds(first + 1, pairs, stride=2), :]
    )

    def keep(a, b):
        return (jnp.abs(off + b - a) < noff).astype(jnp.float32)

    keeps = {(a, b): keep(a, b) for a in (-1, 0, 1) for b in (-1, 0, 1)}

    def band(col):
        return -1 if col < 0 else 1 if col >= tile else 0

    def activate(l, group, x, start):
        lo, hi = (band(c) for c in columns(group, halos[l], 2**l))
        size = x.shape[0]
        for a, begin, end in ((-1, 0, edge), (0, edge, edge + tile), (1, edge + tile, rows)):
            begin, end = max(begin, start), min(end, start + size)
            if begin >= end:
                continue
            g = gelu(x[begin - start : end - start])
            if (a, lo, hi) != (0, 0, 0):
                g = g * pick(keeps[a, lo], keeps[a, hi])
            g_ref[group, BASE + begin : BASE + end, :] = g

    def mirror(l):
        halo, dil = halos[l], 2**l
        groups = (tile + 2 * halo) // 2
        deep = -(-halo // 8) * 8
        top, mid, bot = BASE, BASE + edge, BASE + edge + tile

        def write_bottom(group, c1, c2, limit):
            if c1 >= limit:
                return
            lo = z_ref[(c1 + edge) * edge : (c1 + edge) * edge + deep, :]
            if c2 < limit:
                hi = z_ref[(c2 + edge) * edge : (c2 + edge) * edge + deep, :]
            else:
                hi = g_ref[group, bot : bot + deep, :]
            g_ref[group, bot : bot + deep, :] = pick(lo, hi)

        @pl.when(off == 0)
        def _():
            for k in range(halo):
                group, half = place(tile + k, halo, dil)
                z_ref[pl.ds(k, edge + tile, stride=edge), :] = both(g_ref[group, top:bot, :], half)
            for group in range(groups):
                write_bottom(group, *columns(group, halo, dil), tile)
            for r in range(tile):
                group, half = place(r, halo, dil)
                z_ref[pl.ds(r, edge, stride=tile), :] = both(g_ref[group, top:mid, :], half)
            for group in range(groups):
                c1, c2 = columns(group, halo, dil)
                if c1 < 0:
                    lo = z_ref[(c1 + edge) * tile : (c1 + edge + 1) * tile, :]
                    if c2 < 0:
                        hi = z_ref[(c2 + edge) * tile : (c2 + edge + 1) * tile, :]
                    else:
                        hi = g_ref[group, mid:bot, :]
                    g_ref[group, mid:bot, :] = pick(lo, hi)

        @pl.when(off == 1)
        def _():
            for k in range(halo):
                group, half = place(k, halo, dil)
                z_ref[pl.ds(k, edge, stride=edge), :] = both(g_ref[group, bot - edge : bot, :], half)
            for group in range(groups):
                write_bottom(group, *columns(group, halo, dil), 0)

    for group in range(pairs):
        x = row_bins + col_bins[group : group + 1]
        x_ref[0, group, :, :] = x
        activate(0, group, x, 0)

    for l in range(layers):
        dil = 2**l
        start = (edge - halos[l + 1]) // 8 * 8
        size = rows - 2 * start
        groups = (tile + 2 * halos[l]) // 2
        if l:
            mirror(l)
        for group in range(groups):
            for i in range(3):
                begin = BASE + start + (i - 1) * dil
                h_ref[i, group, 0:size, :] = g_ref[group, begin : begin + size, :].astype(jnp.bfloat16)
        blocks = [(j, e) for j in range((tile + 2 * halos[l + 1]) // (4 * dil)) for e in range(dil)]
        bias = cb_ref[l : l + 1, :]
        now, later = l % 2, (l + 1) % 2
        done = {}
        for at in range(0, len(blocks), GROUP):
            some = blocks[at : at + GROUP]
            lhs = jnp.concatenate(
                [
                    jnp.concatenate(
                        [h_ref[i, (2 * j + s) * dil + e, 0:size, :] for i in range(3) for s in range(3)], axis=1
                    )
                    for j, e in some
                ],
                axis=0,
            )
            acc = jnp.dot(lhs, t_refs[l][...], preferred_element_type=jnp.float32)
            for n, (j, e) in enumerate(some):
                old = [x_ref[now, (2 * j + s) * dil + e, start : start + size, :] for s in range(3)]
                carried = (
                    pick(pltpu.roll(old[0], ch, 1), old[1]),
                    pick(old[1], pltpu.roll(old[2], ch, 1)),
                )
                for s in range(2):
                    x = acc[n * size : (n + 1) * size, s * wide : (s + 1) * wide] + carried[s] + bias
                    group = j * 2 * dil + e + s * dil
                    if l + 1 < layers:
                        x_ref[later, group, start : start + size, :] = x
                        activate(l + 1, group, x, start)
                    else:
                        x_ref[later, group, start : start + size, :] = x
    final = layers % 2
    stretch = 2**layers
    for j in range(tile // (2 * stretch)):
        for e in range(0, stretch, 2):
            even, odd = (
                x_ref[final, j * stretch + e + s, edge : edge + tile, :] for s in range(2)
            )
            col = 2 * stretch * j + e
            out_ref[:, col * ch : (col + 2) * ch] = pick(even, pltpu.roll(odd, ch, 1)).astype(out_ref.dtype)
            col += stretch
            out_ref[:, col * ch : (col + 2) * ch] = pick(pltpu.roll(even, ch, 1), odd).astype(out_ref.dtype)


def tile_call(npos, noff, order, layers, block_slot, table, proj_weight, proj_bias, conv_bias, banded):
    tile = table.shape[1]
    ch = proj_weight.shape[0] // 2
    vmem = pl.BlockSpec(memory_space=pltpu.VMEM)
    wide = 2 * ch
    groups = tile // 2 + 2**layers - 1
    high = tile + 32
    return pl.pallas_call(
        functools.partial(tile_kernel, (layers, tile, ch, npos, noff, order)),
        out_shape=jax.ShapeDtypeStruct((tile, tile * ch), jnp.bfloat16),
        in_specs=[pl.BlockSpec(memory_space=pltpu.SMEM)]
        + [vmem] * (4 + layers),
        out_specs=vmem,
        scratch_shapes=[
            pltpu.VMEM((2, groups, high, wide), jnp.float32),
            pltpu.VMEM((groups, high + 2 * BASE, wide), jnp.float32),
            pltpu.VMEM((3, groups, high, wide), jnp.bfloat16),
            pltpu.VMEM((16 * (tile + 16), wide), jnp.float32),
            pltpu.VMEM((high, wide), jnp.float32),
        ],
        compiler_params=pltpu.CompilerParams(vmem_limit_bytes=48 * 1024 * 1024),
        cost_estimate=pl.CostEstimate(flops=8000000000, bytes_accessed=4000000, transcendentals=2000000),
    )(block_slot, table, proj_weight, proj_bias, conv_bias, *banded)


def parameters_kernel(emb_ref, pw_ref, pb_ref, cb_ref, own_ref, pw2_ref, pb2_ref, cb2_ref):
    own_ref[0] = emb_ref[...]
    for ref, to, axis in ((pw_ref, pw2_ref, 0), (pb_ref, pb2_ref, 1), (cb_ref, cb2_ref, 1)):
        to[...] = jnp.concatenate([ref[...]] * 2, axis=axis)


def parameters_call(bin_embed, proj_weight, proj_bias, conv_bias):
    vmem = pl.BlockSpec(memory_space=pltpu.VMEM)
    ch, emb = proj_weight.shape
    return pl.pallas_call(
        parameters_kernel,
        out_shape=(
            jax.ShapeDtypeStruct((1,) + bin_embed.shape, bin_embed.dtype),
            jax.ShapeDtypeStruct((2 * ch, emb), proj_weight.dtype),
            jax.ShapeDtypeStruct((1, 2 * ch), proj_bias.dtype),
            jax.ShapeDtypeStruct((conv_bias.shape[0], 2 * ch), conv_bias.dtype),
        ),
        in_specs=[vmem] * 4,
        out_specs=(vmem,) * 4,
        cost_estimate=pl.CostEstimate(flops=1000000, bytes_accessed=1000000, transcendentals=0),
    )(bin_embed, proj_weight, proj_bias, conv_bias)


def band_call(weight):
    ch, taps = weight.shape
    vmem = pl.BlockSpec(memory_space=pltpu.VMEM)
    return pl.pallas_call(
        functools.partial(weights_kernel, ch),
        out_shape=jax.ShapeDtypeStruct((2 * taps, 4 * ch), weight.dtype),
        in_specs=[vmem],
        out_specs=vmem,
        cost_estimate=pl.CostEstimate(flops=1000000, bytes_accessed=1000000, transcendentals=0),
    )(weight)


def on_device(bin_embed, block_slot, proj_weight, proj_bias, conv_weight, conv_bias):
    npos, noff = lax.axis_size("pos"), lax.axis_size("off")
    tile, emb = bin_embed.shape
    layers, taps, ch = conv_weight.shape
    bits = npos.bit_length() - 1
    order = tuple(reversed(range(bits)))
    turned = jnp.swapaxes(conv_weight, 1, 2)
    zero = lax.optimization_barrier(jnp.zeros((1,), block_slot.dtype))
    table = bin_embed[None]
    weights, banded, bands = [turned[l] for l in range(layers)], [], [0, 2, 2]
    for stage, bit in enumerate(order):
        there = lax.ppermute(table, "pos", [(i, i ^ (1 << bit)) for i in range(npos)])
        if stage == 0:
            table, *small = parameters_call(bin_embed, proj_weight.T, proj_bias[None], conv_bias)
            slots = jnp.maximum(block_slot, zero)
            there, table, small, slots, weights = lax.optimization_barrier((there, table, small, slots, weights))
        else:
            count = bands[stage] if stage < len(bands) else 0
            made = [band_call(weight) for weight in weights[:count]]
            there, made, weights = lax.optimization_barrier((there, made, weights[count:]))
            banded += made
        table = jnp.concatenate([table, there], axis=0)
    banded += [band_call(weight) for weight in weights]
    out = tile_call(npos, noff, order, layers, slots, table, *small, banded)
    return out.reshape(1, 1, tile, tile * ch)


def solution(mesh):
    placed = (P("pos", None), P(), P(), P(), P(), P())
    return jax.shard_map(
        on_device,
        mesh=mesh,
        in_specs=placed,
        out_specs=P("pos", "off", None, None),
        check_vma=False,
    )
```

```python
import functools

import jax
import jax.numpy as jnp
from jax import lax
from jax.experimental import pallas as pl
from jax.experimental.pallas import tpu as pltpu
from jax.sharding import PartitionSpec as P

GROUP = 4
BASE = 8


def gelu(x):
    u = x * (0.7978845608028654 + 0.035677408136300125 * (x * x))
    half = 0.5 * x
    return half + half * jnp.tanh(u)


def place(col, halo, dil):
    u = col + halo
    within = u % (2 * dil)
    return (u // (2 * dil)) * dil + within % dil, within // dil


def columns(group, halo, dil):
    first = (group // dil) * 2 * dil + group % dil - halo
    return first, first + dil


def weights_kernel(ch, which, cw_ref, *t_refs):
    zero = jnp.zeros((ch, ch), cw_ref.dtype)
    for l, t_ref in zip(which, t_refs):
        taps = jnp.transpose(cw_ref[l].astype(jnp.float32)).astype(t_ref.dtype)
        for i in range(3):
            for a in range(6):
                row = [
                    taps[(3 * i + a - b) * ch : (3 * i + a - b + 1) * ch] if 0 <= a - b <= 2 else zero
                    for b in (0, 2, 1, 3)
                ]
                t_ref[(6 * i + a) * ch : (6 * i + a + 1) * ch, :] = jnp.concatenate(row, axis=1)


def tile_kernel(
    dims, slot_ref, emb_ref, pw_ref, pb_ref, cb_ref, *refs
):
    t_refs, (out_ref, x_ref, g_ref, h_ref, z_ref, bins_ref) = refs[: dims[0]], refs[dims[0] :]
    layers, tile, ch, npos, noff, order = dims
    wide = 2 * ch
    edge = 16
    rows = tile + 2 * edge
    halos = [2**layers - 2**l for l in range(layers + 1)]
    me, off = lax.axis_index("pos"), lax.axis_index("off")
    low = lax.broadcasted_iota(jnp.int32, (1, wide), 1) < ch

    def pick(lo, hi):
        return jnp.where(low, lo, hi)

    def both(value, half):
        turned = pltpu.roll(value, ch, 1)
        return pick(turned, value) if half else pick(value, turned)

    def block(b):
        away = jnp.bitwise_xor(slot_ref[lax.rem(b + npos, npos)], me)
        index = 0
        for place_in, bit in enumerate(order):
            index += jnp.bitwise_and(lax.shift_right_logical(away, bit), 1) << place_in
        return index

    pw = pw_ref[...]

    def bins(b):
        first, here, last = (emb_ref[block(b + k)] for k in (-1, 0, 1))
        picked = jnp.concatenate([first[tile - edge :], here, last[:edge]], axis=0)
        made = lax.dot_general(picked, pw, (((1,), (1,)), ((), ())), preferred_element_type=jnp.float32)
        return made.astype(jnp.bfloat16).astype(jnp.float32)

    row_bins = bins(me) + pb_ref[...]
    bins_ref[...] = bins(me + off)
    pairs = (tile + 2 * halos[0]) // 2
    first = edge - halos[0]
    col_bins = pick(
        bins_ref[pl.ds(first, pairs, stride=2), :], bins_ref[pl.ds(first + 1, pairs, stride=2), :]
    )

    def keep(a, b):
        return (jnp.abs(off + b - a) < noff).astype(jnp.float32)

    keeps = {(a, b): keep(a, b) for a in (-1, 0, 1) for b in (-1, 0, 1)}

    def band(col):
        return -1 if col < 0 else 1 if col >= tile else 0

    def activate(l, group, x, start):
        lo, hi = (band(c) for c in columns(group, halos[l], 2**l))
        size = x.shape[0]
        for a, begin, end in ((-1, 0, edge), (0, edge, edge + tile), (1, edge + tile, rows)):
            begin, end = max(begin, start), min(end, start + size)
            if begin >= end:
                continue
            g = gelu(x[begin - start : end - start])
            if (a, lo, hi) != (0, 0, 0):
                g = g * pick(keeps[a, lo], keeps[a, hi])
            g_ref[group, BASE + begin : BASE + end, :] = g

    def mirror(l):
        halo, dil = halos[l], 2**l
        groups = (tile + 2 * halo) // 2
        deep = -(-halo // 8) * 8
        top, mid, bot = BASE, BASE + edge, BASE + edge + tile

        def write_bottom(group, c1, c2, limit):
            if c1 >= limit:
                return
            lo = z_ref[(c1 + edge) * edge : (c1 + edge) * edge + deep, :]
            if c2 < limit:
                hi = z_ref[(c2 + edge) * edge : (c2 + edge) * edge + deep, :]
            else:
                hi = g_ref[group, bot : bot + deep, :]
            g_ref[group, bot : bot + deep, :] = pick(lo, hi)

        @pl.when(off == 0)
        def _():
            for k in range(halo):
                group, half = place(tile + k, halo, dil)
                z_ref[pl.ds(k, edge + tile, stride=edge), :] = both(g_ref[group, top:bot, :], half)
            for group in range(groups):
                write_bottom(group, *columns(group, halo, dil), tile)
            for r in range(tile):
                group, half = place(r, halo, dil)
                z_ref[pl.ds(r, edge, stride=tile), :] = both(g_ref[group, top:mid, :], half)
            for group in range(groups):
                c1, c2 = columns(group, halo, dil)
                if c1 < 0:
                    lo = z_ref[(c1 + edge) * tile : (c1 + edge + 1) * tile, :]
                    if c2 < 0:
                        hi = z_ref[(c2 + edge) * tile : (c2 + edge + 1) * tile, :]
                    else:
                        hi = g_ref[group, mid:bot, :]
                    g_ref[group, mid:bot, :] = pick(lo, hi)

        @pl.when(off == 1)
        def _():
            for k in range(halo):
                group, half = place(k, halo, dil)
                z_ref[pl.ds(k, edge, stride=edge), :] = both(g_ref[group, bot - edge : bot, :], half)
            for group in range(groups):
                write_bottom(group, *columns(group, halo, dil), 0)

    for group in range(pairs):
        x = row_bins + col_bins[group : group + 1]
        x_ref[0, group, :, :] = x
        activate(0, group, x, 0)

    for l in range(layers):
        dil = 2**l
        start = (edge - halos[l + 1]) // 8 * 8
        size = rows - 2 * start
        groups = (tile + 2 * halos[l]) // 2
        if l:
            mirror(l)
        for group in range(groups):
            for i in range(3):
                begin = BASE + start + (i - 1) * dil
                h_ref[i, group, 0:size, :] = g_ref[group, begin : begin + size, :].astype(jnp.bfloat16)
        blocks = [(j, e) for j in range((tile + 2 * halos[l + 1]) // (4 * dil)) for e in range(dil)]
        bias = cb_ref[l : l + 1, :]
        now, later = l % 2, (l + 1) % 2
        done = {}
        for at in range(0, len(blocks), GROUP):
            some = blocks[at : at + GROUP]
            lhs = jnp.concatenate(
                [
                    jnp.concatenate(
                        [h_ref[i, (2 * j + s) * dil + e, 0:size, :] for i in range(3) for s in range(3)], axis=1
                    )
                    for j, e in some
                ],
                axis=0,
            )
            acc = jnp.dot(lhs, t_refs[l][...], preferred_element_type=jnp.float32)
            for n, (j, e) in enumerate(some):
                old = [x_ref[now, (2 * j + s) * dil + e, start : start + size, :] for s in range(3)]
                carried = (
                    pick(pltpu.roll(old[0], ch, 1), old[1]),
                    pick(old[1], pltpu.roll(old[2], ch, 1)),
                )
                for s in range(2):
                    x = acc[n * size : (n + 1) * size, s * wide : (s + 1) * wide] + carried[s] + bias
                    group = j * 2 * dil + e + s * dil
                    if l + 1 < layers:
                        x_ref[later, group, start : start + size, :] = x
                        activate(l + 1, group, x, start)
                    else:
                        x_ref[later, group, start : start + size, :] = x
    final = layers % 2
    stretch = 2**layers
    for j in range(tile // (2 * stretch)):
        for e in range(0, stretch, 2):
            even, odd = (
                x_ref[final, j * stretch + e + s, edge : edge + tile, :] for s in range(2)
            )
            col = 2 * stretch * j + e
            out_ref[:, col * ch : (col + 2) * ch] = pick(even, pltpu.roll(odd, ch, 1)).astype(out_ref.dtype)
            col += stretch
            out_ref[:, col * ch : (col + 2) * ch] = pick(pltpu.roll(even, ch, 1), odd).astype(out_ref.dtype)


def tile_call(npos, noff, order, layers, block_slot, table, proj_weight, proj_bias, conv_bias, banded):
    tile = table.shape[1]
    ch = proj_weight.shape[0] // 2
    vmem = pl.BlockSpec(memory_space=pltpu.VMEM)
    wide = 2 * ch
    groups = tile // 2 + 2**layers - 1
    high = tile + 32
    return pl.pallas_call(
        functools.partial(tile_kernel, (layers, tile, ch, npos, noff, order)),
        out_shape=jax.ShapeDtypeStruct((tile, tile * ch), jnp.bfloat16),
        in_specs=[pl.BlockSpec(memory_space=pltpu.SMEM)]
        + [vmem] * (4 + layers),
        out_specs=vmem,
        scratch_shapes=[
            pltpu.VMEM((2, groups, high, wide), jnp.float32),
            pltpu.VMEM((groups, high + 2 * BASE, wide), jnp.float32),
            pltpu.VMEM((3, groups, high, wide), jnp.bfloat16),
            pltpu.VMEM((16 * (tile + 16), wide), jnp.float32),
            pltpu.VMEM((high, wide), jnp.float32),
        ],
        compiler_params=pltpu.CompilerParams(vmem_limit_bytes=48 * 1024 * 1024),
        cost_estimate=pl.CostEstimate(flops=8000000000, bytes_accessed=4000000, transcendentals=2000000),
    )(block_slot, table, proj_weight, proj_bias, conv_bias, *banded)


def parameters_kernel(emb_ref, pw_ref, pb_ref, cb_ref, cw_ref, own_ref, pw2_ref, pb2_ref, cb2_ref, cw2_ref):
    own_ref[0] = emb_ref[...]
    cw2_ref[...] = cw_ref[...]
    for ref, to, axis in ((pw_ref, pw2_ref, 0), (pb_ref, pb2_ref, 1), (cb_ref, cb2_ref, 1)):
        to[...] = jnp.concatenate([ref[...]] * 2, axis=axis)


def parameters_call(bin_embed, proj_weight, proj_bias, conv_bias, weights):
    vmem = pl.BlockSpec(memory_space=pltpu.VMEM)
    ch, emb = proj_weight.shape
    return pl.pallas_call(
        parameters_kernel,
        out_shape=(
            pltpu.VMEM((1,) + bin_embed.shape, bin_embed.dtype),
            pltpu.VMEM((2 * ch, emb), proj_weight.dtype),
            pltpu.VMEM((1, 2 * ch), proj_bias.dtype),
            pltpu.VMEM((conv_bias.shape[0], 2 * ch), conv_bias.dtype),
            pltpu.VMEM(weights.shape, weights.dtype),
        ),
        in_specs=[vmem] * 5,
        out_specs=(vmem,) * 5,
        cost_estimate=pl.CostEstimate(flops=1000000, bytes_accessed=1000000, transcendentals=0),
    )(bin_embed, proj_weight, proj_bias, conv_bias, weights)


def band_call(weights, which):
    layers, ch, taps = weights.shape
    vmem = pl.BlockSpec(memory_space=pltpu.VMEM)
    return pl.pallas_call(
        functools.partial(weights_kernel, ch, which),
        out_shape=(pltpu.VMEM((2 * taps, 4 * ch), weights.dtype),) * len(which),
        in_specs=[vmem],
        out_specs=(vmem,) * len(which),
        cost_estimate=pl.CostEstimate(flops=1000000, bytes_accessed=1000000, transcendentals=0),
    )(weights)


def on_device(bin_embed, block_slot, proj_weight, proj_bias, conv_weight, conv_bias):
    npos, noff = lax.axis_size("pos"), lax.axis_size("off")
    tile, emb = bin_embed.shape
    layers, taps, ch = conv_weight.shape
    bits = npos.bit_length() - 1
    order = tuple(reversed(range(bits)))
    turned = jnp.swapaxes(conv_weight, 1, 2)
    zero = lax.optimization_barrier(jnp.zeros((1,), block_slot.dtype))
    table = bin_embed[None]
    banded, todo = [], tuple(range(layers))
    for stage, bit in enumerate(order):
        there = lax.ppermute(table, "pos", [(i, i ^ (1 << bit)) for i in range(npos)])
        if stage == 0:
            table, *small, turned = parameters_call(bin_embed, proj_weight.T, proj_bias[None], conv_bias, turned)
            slots = jnp.maximum(block_slot, zero)
            there, table, small, slots, turned = lax.optimization_barrier((there, table, small, slots, turned))
        elif todo:
            made = band_call(turned, todo[:2])
            there, made, turned = lax.optimization_barrier((there, made, turned))
            banded, todo = banded + list(made), todo[2:]
        table = jnp.concatenate([table, there], axis=0)
    if todo:
        banded += band_call(turned, todo)
    out = tile_call(npos, noff, order, layers, slots, table, *small, banded)
    return out.reshape(1, 1, tile, tile * ch)


def solution(mesh):
    placed = (P("pos", None), P(), P(), P(), P(), P())
    return jax.shard_map(
        on_device,
        mesh=mesh,
        in_specs=placed,
        out_specs=P("pos", "off", None, None),
        check_vma=False,
    )
```

```python
import functools

import jax
import jax.numpy as jnp
from jax import lax
from jax.experimental import pallas as pl
from jax.experimental.pallas import tpu as pltpu
from jax.sharding import PartitionSpec as P

GROUP = 4
BASE = 8
EDGE = 16


def gelu(x):
    u = x * (0.7978845608028654 + 0.035677408136300125 * (x * x))
    half = 0.5 * x
    return half + half * jnp.tanh(u)


def place(col, halo, dil):
    u = col + halo
    within = u % (2 * dil)
    return (u // (2 * dil)) * dil + within % dil, within // dil


def columns(group, halo, dil):
    first = (group // dil) * 2 * dil + group % dil - halo
    return first, first + dil


def weights_kernel(ch, which, cw_ref, *t_refs):
    zero = jnp.zeros((ch, ch), cw_ref.dtype)
    for l, t_ref in zip(which, t_refs):
        taps = jnp.transpose(cw_ref[l].astype(jnp.float32)).astype(t_ref.dtype)
        for i in range(3):
            for a in range(6):
                row = [
                    taps[(3 * i + a - b) * ch : (3 * i + a - b + 1) * ch] if 0 <= a - b <= 2 else zero
                    for b in (0, 2, 1, 3)
                ]
                t_ref[(6 * i + a) * ch : (6 * i + a + 1) * ch, :] = jnp.concatenate(row, axis=1)


def tile_kernel(dims, slot_ref, emb_ref, pw_ref, pb_ref, cb_ref, *refs):
    layers, tile, ch, npos, noff, order = dims
    t_refs = refs[:layers]
    out_ref, x_ref, g_ref, side_ref, left_ref, corner_ref, bins_ref, made_ref, sems = refs[layers:]
    wide = 2 * ch
    edge = EDGE
    rows = tile + 2 * edge
    halos = [2**layers - 2**l for l in range(layers + 1)]
    top, mid, bot = BASE, BASE + edge, BASE + edge + tile
    side_step, left_step = edge + 1, tile + 1
    me, off = lax.axis_index("pos"), lax.axis_index("off")
    low = lax.broadcasted_iota(jnp.int32, (1, wide), 1) < ch
    diagonal, beside = off == 0, off == 1

    def pick(lo, hi):
        return jnp.where(low, lo, hi)

    def both(value):
        turned = pltpu.roll(value, ch, 1)
        return pick(value, turned), pick(turned, value)

    def block(b):
        slot = slot_ref[lax.rem(b + npos, npos)]
        if not order:
            return slot
        away = jnp.bitwise_xor(slot, me)
        bits = [jnp.bitwise_and(lax.shift_right_logical(away, bit), 1) for bit in order]
        for bit in bits[:-1]:
            bits[-1] = jnp.bitwise_xor(bits[-1], bit)
        return sum(bit << n for n, bit in enumerate(bits))

    pw = pw_ref[...]

    def bins(b):
        first, here, last = (emb_ref[block(b + k)] for k in (-1, 0, 1))
        picked = jnp.concatenate([first[tile - edge :], here, last[:edge]], axis=0)
        made = lax.dot_general(picked, pw, (((1,), (1,)), ((), ())), preferred_element_type=jnp.float32)
        return made.astype(jnp.bfloat16).astype(jnp.float32)

    row_bins = bins(me) + pb_ref[...]
    bins_ref[...] = bins(me + off)
    pairs = (tile + 2 * halos[0]) // 2
    first = edge - halos[0]
    col_bins = pick(
        bins_ref[pl.ds(first, pairs, stride=2), :], bins_ref[pl.ds(first + 1, pairs, stride=2), :]
    )

    keeps = {
        (a, b): (jnp.abs(off + b - a) < noff).astype(jnp.float32) for a in (-1, 0, 1) for b in (-1, 0, 1)
    }

    def band(col):
        return -1 if col < 0 else 1 if col >= tile else 0

    ready = [set() for _ in range(layers)]
    seen = [set() for _ in range(layers)]
    waiting = [[] for _ in range(layers)]

    def activate(l, group, x, start):
        lo, hi = (band(c) for c in columns(group, halos[l], 2**l))
        size = x.shape[0]
        for a, begin, end in ((-1, 0, edge), (0, edge, edge + tile), (1, edge + tile, rows)):
            begin, end = max(begin, start), min(end, start + size)
            if begin < end:
                g = gelu(x[begin - start : end - start])
                if (a, lo, hi) != (0, 0, 0):
                    g = g * pick(keeps[a, lo], keeps[a, hi])
                g_ref[group, BASE + begin : BASE + end, :] = g

    def mirror(l, group):
        halo, dil = halos[l], 2**l
        deep = -(-halo // 8) * 8
        cols = columns(group, halo, dil)
        seen[l].update(cols)
        if any(tile <= c < tile + halo for c in cols):
            for c, value in zip(cols, both(g_ref[group, top:bot, :])):
                if c >= tile:
                    side_ref[pl.ds(c - tile, edge + tile, stride=side_step), :] = value
        if any(0 <= c < tile for c in cols):
            for c, value in zip(cols, both(g_ref[group, top:mid, :])):
                if 0 <= c < tile:
                    left_ref[pl.ds(c, edge, stride=left_step), :] = value
        if any(0 <= c < halo for c in cols):
            for c, value in zip(cols, both(g_ref[group, bot - edge : bot, :])):
                if 0 <= c < halo:
                    corner_ref[pl.ds(c, edge, stride=side_step), :] = value
        waiting[l].append(group)
        for group in list(waiting[l]):
            c1, c2 = columns(group, halo, dil)
            if c1 < tile and not seen[l].issuperset(range(tile, tile + halo)):
                continue
            if c1 < 0 and not seen[l].issuperset(range(tile)):
                continue
            waiting[l].remove(group)
            ready[l].add(group)
            if c1 < tile:
                now = g_ref[group, bot : bot + deep, :]
                at = [(c + edge) * side_step for c in (c1, c2)]
                made = [side_ref[k : k + deep, :] if c < tile else now for c, k in zip((c1, c2), at)]
                new = jnp.where(diagonal, pick(*made), now)
                if c1 < 0:
                    made = [corner_ref[k : k + deep, :] if c < 0 else now for c, k in zip((c1, c2), at)]
                    new = jnp.where(beside, pick(*made), new)
                g_ref[group, bot : bot + deep, :] = new
            if c1 < 0:
                now = g_ref[group, mid:bot, :]
                at = [(c + edge) * left_step for c in (c1, c2)]
                made = [left_ref[k : k + tile, :] if c < 0 else now for c, k in zip((c1, c2), at)]
                g_ref[group, mid:bot, :] = jnp.where(diagonal, pick(*made), now)

    def begin(group):
        x = row_bins + col_bins[group : group + 1]
        x_ref[0, group, :, :] = x
        activate(0, group, x, 0)
        ready[0].add(group)

    stretch = 2**layers
    span = 2 * stretch * ch

    def send(j):
        here = (slice(None), pl.ds(j * span, span))
        return pltpu.make_async_copy(made_ref.at[here], out_ref.at[here], sems.at[j])

    def finish(l, some, acc):
        dil = 2**l
        start = (edge - halos[l + 1]) // 8 * 8
        size = rows - 2 * start
        for n, (j, e) in enumerate(some):
            old = [x_ref[l % 2, (2 * j + s) * dil + e, start : start + size, :] for s in range(3)]
            carried = (pick(pltpu.roll(old[0], ch, 1), old[1]), pick(old[1], pltpu.roll(old[2], ch, 1)))
            new = [
                acc[n * size : (n + 1) * size, s * wide : (s + 1) * wide] + carried[s] + cb_ref[l : l + 1, :]
                for s in range(2)
            ]
            if l + 1 < layers:
                for s, x in enumerate(new):
                    group = j * 2 * dil + e + s * dil
                    x_ref[(l + 1) % 2, group, start : start + size, :] = x
                    activate(l + 1, group, x, start)
                    mirror(l + 1, group)
            elif e % 2 == 0:
                even = new
            else:
                for s in range(2):
                    col = (stretch * 2 * j + e - 1 + s * dil) * ch
                    value = pick(even[s], pltpu.roll(new[s], ch, 1))
                    made_ref[:, col : col + wide] = value.astype(made_ref.dtype)
                    col += stretch * ch
                    value = pick(pltpu.roll(even[s], ch, 1), new[s])
                    made_ref[:, col : col + wide] = value.astype(made_ref.dtype)
                if e == dil - 1:
                    send(j).start()

    unfinished = None
    for l in range(layers):
        dil = 2**l
        start = (edge - halos[l + 1]) // 8 * 8
        size = rows - 2 * start
        count = (tile + 2 * halos[l + 1]) // (4 * dil)
        blocks = [(j, e) for j in reversed(range(count)) for e in range(dil)]
        for at in range(0, len(blocks), GROUP):
            some = blocks[at : at + GROUP]
            need = [(2 * j + s) * dil + e for j, e in some for s in range(3)]
            if l == 0:
                for group in need:
                    if group not in ready[0]:
                        begin(group)
            if not ready[l].issuperset(need):
                finish(*unfinished)
                unfinished = None
            assert ready[l].issuperset(need)

            def taps(j, e):
                return [
                    g_ref[(2 * j + s) * dil + e, BASE + start + i * dil : BASE + start + i * dil + size, :].astype(
                        jnp.bfloat16
                    )
                    for i in (-1, 0, 1)
                    for s in range(3)
                ]

            lhs = jnp.concatenate([jnp.concatenate(taps(j, e), axis=1) for j, e in some], axis=0)
            acc = jnp.dot(lhs, t_refs[l][...], preferred_element_type=jnp.float32)
            if unfinished:
                finish(*unfinished)
            unfinished = (l, some, acc)
    finish(*unfinished)
    for j in range(tile // (2 * stretch)):
        send(j).wait()


def tile_call(npos, noff, order, layers, block_slot, table, proj_weight, proj_bias, conv_bias, banded):
    tile = table.shape[1]
    ch = proj_weight.shape[0] // 2
    vmem = pl.BlockSpec(memory_space=pltpu.VMEM)
    wide = 2 * ch
    groups = tile // 2 + 2**layers - 1
    high = tile + 2 * EDGE
    return pl.pallas_call(
        functools.partial(tile_kernel, (layers, tile, ch, npos, noff, order)),
        out_shape=jax.ShapeDtypeStruct((tile, tile * ch), jnp.bfloat16),
        in_specs=[pl.BlockSpec(memory_space=pltpu.SMEM)]
        + [vmem] * (4 + layers),
        out_specs=pl.BlockSpec(memory_space=pl.ANY),
        scratch_shapes=[
            pltpu.VMEM((2, groups, high, wide), jnp.float32),
            pltpu.VMEM((groups, high + 2 * BASE, wide), jnp.float32),
            pltpu.VMEM(((EDGE + 1) * (EDGE + tile), wide), jnp.float32),
            pltpu.VMEM(((tile + 1) * EDGE, wide), jnp.float32),
            pltpu.VMEM(((EDGE + 1) * EDGE, wide), jnp.float32),
            pltpu.VMEM((high, wide), jnp.float32),
            pltpu.VMEM((tile, tile * ch), jnp.bfloat16),
            pltpu.SemaphoreType.DMA((tile // 2 ** (layers + 1),)),
        ],
        compiler_params=pltpu.CompilerParams(vmem_limit_bytes=48 * 1024 * 1024),
        cost_estimate=pl.CostEstimate(flops=8000000000, bytes_accessed=4000000, transcendentals=2000000),
    )(block_slot, table, proj_weight, proj_bias, conv_bias, *banded)


def parameters_kernel(emb_ref, pw_ref, pb_ref, cb_ref, cw_ref, own_ref, pw2_ref, pb2_ref, cb2_ref, cw2_ref):
    own_ref[0] = emb_ref[...]
    cw2_ref[...] = cw_ref[...]
    for ref, to, axis in ((pw_ref, pw2_ref, 0), (pb_ref, pb2_ref, 1), (cb_ref, cb2_ref, 1)):
        to[...] = jnp.concatenate([ref[...]] * 2, axis=axis)


def parameters_call(bin_embed, proj_weight, proj_bias, conv_bias, weights):
    vmem = pl.BlockSpec(memory_space=pltpu.VMEM)
    ch, emb = proj_weight.shape
    return pl.pallas_call(
        parameters_kernel,
        out_shape=(
            pltpu.VMEM((1,) + bin_embed.shape, bin_embed.dtype),
            pltpu.VMEM((2 * ch, emb), proj_weight.dtype),
            pltpu.VMEM((1, 2 * ch), proj_bias.dtype),
            pltpu.VMEM((conv_bias.shape[0], 2 * ch), conv_bias.dtype),
            pltpu.VMEM(weights.shape, weights.dtype),
        ),
        in_specs=[vmem] * 5,
        out_specs=(vmem,) * 5,
        cost_estimate=pl.CostEstimate(flops=1000000, bytes_accessed=1000000, transcendentals=0),
    )(bin_embed, proj_weight, proj_bias, conv_bias, weights)


def band_call(weights, which):
    layers, ch, taps = weights.shape
    vmem = pl.BlockSpec(memory_space=pltpu.VMEM)
    return pl.pallas_call(
        functools.partial(weights_kernel, ch, which),
        out_shape=(pltpu.VMEM((2 * taps, 4 * ch), weights.dtype),) * len(which),
        in_specs=[vmem],
        out_specs=(vmem,) * len(which),
        cost_estimate=pl.CostEstimate(flops=1000000, bytes_accessed=1000000, transcendentals=0),
    )(weights)


def on_device(bin_embed, block_slot, proj_weight, proj_bias, conv_weight, conv_bias):
    npos, noff = lax.axis_size("pos"), lax.axis_size("off")
    tile, emb = bin_embed.shape
    layers, taps, ch = conv_weight.shape
    order = tuple(reversed(range(npos.bit_length() - 1))) if npos & (npos - 1) == 0 else ()
    turned = jnp.swapaxes(conv_weight, 1, 2)
    zero = lax.optimization_barrier(jnp.zeros((1,), block_slot.dtype))
    table = bin_embed[None]
    banded, todo = [], tuple(range(layers))
    for stage, bit in enumerate(order):
        there = lax.ppermute(table, "pos", [(i, i ^ (1 << bit | 1)) for i in range(npos)])
        if stage == 0:
            table, *small, turned = parameters_call(bin_embed, proj_weight.T, proj_bias[None], conv_bias, turned)
            slots = jnp.maximum(block_slot, zero)
            there, table, small, slots, turned = lax.optimization_barrier((there, table, small, slots, turned))
        elif todo:
            made = band_call(turned, todo[:2])
            there, made, turned = lax.optimization_barrier((there, made, turned))
            banded, todo = banded + list(made), todo[2:]
        table = jnp.concatenate([table, there], axis=0)
    if not order:
        _, *small, turned = parameters_call(bin_embed, proj_weight.T, proj_bias[None], conv_bias, turned)
        table, slots = lax.all_gather(bin_embed, "pos"), block_slot
    if todo:
        banded += band_call(turned, todo)
    out = tile_call(npos, noff, order, layers, slots, table, *small, banded)
    return out.reshape(1, 1, tile, tile * ch)


def solution(mesh):
    placed = (P("pos", None), P(), P(), P(), P(), P())
    return jax.shard_map(
        on_device,
        mesh=mesh,
        in_specs=placed,
        out_specs=P("pos", "off", None, None),
        check_vma=False,
    )
```

```python
import functools

import jax
import jax.numpy as jnp
from jax import lax
from jax.experimental import pallas as pl
from jax.experimental.pallas import tpu as pltpu
from jax.sharding import PartitionSpec as P

GROUP = 4
BASE = 8
EDGE = 16


def gelu(x):
    u = x * (0.7978845608028654 + 0.035677408136300125 * (x * x))
    half = 0.5 * x
    return half + half * jnp.tanh(u)


def place(col, halo, dil):
    u = col + halo
    within = u % (2 * dil)
    return (u // (2 * dil)) * dil + within % dil, within // dil


def columns(group, halo, dil):
    first = (group // dil) * 2 * dil + group % dil - halo
    return first, first + dil


def weights_kernel(ch, which, cw_ref, *t_refs):
    zero = jnp.zeros((ch, ch), cw_ref.dtype)
    for l, t_ref in zip(which, t_refs):
        taps = jnp.transpose(cw_ref[l].astype(jnp.float32)).astype(t_ref.dtype)
        for i in range(3):
            for a in range(6):
                row = [
                    taps[(3 * i + a - b) * ch : (3 * i + a - b + 1) * ch] if 0 <= a - b <= 2 else zero
                    for b in (0, 2, 1, 3)
                ]
                t_ref[(6 * i + a) * ch : (6 * i + a + 1) * ch, :] = jnp.concatenate(row, axis=1)


def tile_kernel(dims, slot_ref, emb_ref, pw_ref, pb_ref, cb_ref, *refs):
    layers, tile, ch, npos, noff, order = dims
    t_refs = refs[:layers]
    out_ref, x_ref, g_ref, side_ref, left_ref, corner_ref, bins_ref, made_ref, sems = refs[layers:]
    wide = 2 * ch
    edge = EDGE
    rows = tile + 2 * edge
    halos = [2**layers - 2**l for l in range(layers + 1)]
    top, mid, bot = BASE, BASE + edge, BASE + edge + tile
    side_step, left_step = edge + 1, tile + 1
    me, off = lax.axis_index("pos"), lax.axis_index("off")
    low = lax.broadcasted_iota(jnp.int32, (1, wide), 1) < ch
    diagonal, beside = off == 0, off == 1

    def pick(lo, hi):
        return jnp.where(low, lo, hi)

    def both(value):
        turned = pltpu.roll(value, ch, 1)
        return pick(value, turned), pick(turned, value)

    def block(b):
        slot = slot_ref[lax.rem(b + npos, npos)]
        if not order:
            return slot
        away = jnp.bitwise_xor(slot, me)
        bits = [jnp.bitwise_and(lax.shift_right_logical(away, bit), 1) for bit in order]
        for bit in bits[:-1]:
            bits[-1] = jnp.bitwise_xor(bits[-1], bit)
        return sum(bit << n for n, bit in enumerate(bits))

    pw = pw_ref[...]

    def bins(b):
        first, here, last = (emb_ref[block(b + k)] for k in (-1, 0, 1))
        picked = jnp.concatenate([first[tile - edge :], here, last[:edge]], axis=0)
        made = lax.dot_general(picked, pw, (((1,), (1,)), ((), ())), preferred_element_type=jnp.float32)
        return made.astype(jnp.bfloat16).astype(jnp.float32)

    row_bins = bins(me) + pb_ref[...]
    bins_ref[...] = bins(me + off)
    pairs = (tile + 2 * halos[0]) // 2
    first = edge - halos[0]
    col_bins = pick(
        bins_ref[pl.ds(first, pairs, stride=2), :], bins_ref[pl.ds(first + 1, pairs, stride=2), :]
    )

    keeps = {
        (a, b): (jnp.abs(off + b - a) < noff).astype(jnp.float32) for a in (-1, 0, 1) for b in (-1, 0, 1)
    }

    def band(col):
        return -1 if col < 0 else 1 if col >= tile else 0

    ready = [set() for _ in range(layers)]
    seen = [set() for _ in range(layers)]
    waiting = [[] for _ in range(layers)]

    def activate(l, group, x, start):
        lo, hi = (band(c) for c in columns(group, halos[l], 2**l))
        size = x.shape[0]
        for a, begin, end in ((-1, 0, edge), (0, edge, edge + tile), (1, edge + tile, rows)):
            begin, end = max(begin, start), min(end, start + size)
            if begin < end:
                g = gelu(x[begin - start : end - start].astype(jnp.bfloat16)).astype(jnp.float32)
                if (a, lo, hi) != (0, 0, 0):
                    g = g * pick(keeps[a, lo], keeps[a, hi])
                g_ref[group, BASE + begin : BASE + end, :] = g

    def mirror(l, group):
        halo, dil = halos[l], 2**l
        deep = -(-halo // 8) * 8
        cols = columns(group, halo, dil)
        seen[l].update(cols)
        if any(tile <= c < tile + halo for c in cols):
            for c, value in zip(cols, both(g_ref[group, top:bot, :])):
                if c >= tile:
                    side_ref[pl.ds(c - tile, edge + tile, stride=side_step), :] = value
        if any(0 <= c < tile for c in cols):
            for c, value in zip(cols, both(g_ref[group, top:mid, :])):
                if 0 <= c < tile:
                    left_ref[pl.ds(c, edge, stride=left_step), :] = value
        if any(0 <= c < halo for c in cols):
            for c, value in zip(cols, both(g_ref[group, bot - edge : bot, :])):
                if 0 <= c < halo:
                    corner_ref[pl.ds(c, edge, stride=side_step), :] = value
        waiting[l].append(group)
        for group in list(waiting[l]):
            c1, c2 = columns(group, halo, dil)
            if c1 < tile and not seen[l].issuperset(range(tile, tile + halo)):
                continue
            if c1 < 0 and not seen[l].issuperset(range(tile)):
                continue
            waiting[l].remove(group)
            ready[l].add(group)
            if c1 < tile:
                now = g_ref[group, bot : bot + deep, :]
                at = [(c + edge) * side_step for c in (c1, c2)]
                made = [side_ref[k : k + deep, :] if c < tile else now for c, k in zip((c1, c2), at)]
                new = jnp.where(diagonal, pick(*made), now)
                if c1 < 0:
                    made = [corner_ref[k : k + deep, :] if c < 0 else now for c, k in zip((c1, c2), at)]
                    new = jnp.where(beside, pick(*made), new)
                g_ref[group, bot : bot + deep, :] = new
            if c1 < 0:
                now = g_ref[group, mid:bot, :]
                at = [(c + edge) * left_step for c in (c1, c2)]
                made = [left_ref[k : k + tile, :] if c < 0 else now for c, k in zip((c1, c2), at)]
                g_ref[group, mid:bot, :] = jnp.where(diagonal, pick(*made), now)

    def begin(group):
        x = row_bins + col_bins[group : group + 1]
        x_ref[0, group, :, :] = x
        activate(0, group, x, 0)
        ready[0].add(group)

    stretch = 2**layers
    span = 2 * stretch * ch

    def send(j):
        here = (slice(None), pl.ds(j * span, span))
        return pltpu.make_async_copy(made_ref.at[here], out_ref.at[here], sems.at[j])

    def finish(l, some, acc):
        dil = 2**l
        start = (edge - halos[l + 1]) // 8 * 8
        size = rows - 2 * start
        for n, (j, e) in enumerate(some):
            old = [x_ref[l % 2, (2 * j + s) * dil + e, start : start + size, :] for s in range(3)]
            carried = (pick(pltpu.roll(old[0], ch, 1), old[1]), pick(old[1], pltpu.roll(old[2], ch, 1)))
            new = [
                acc[n * size : (n + 1) * size, s * wide : (s + 1) * wide] + carried[s] + cb_ref[l : l + 1, :]
                for s in range(2)
            ]
            if l + 1 < layers:
                for s, x in enumerate(new):
                    group = j * 2 * dil + e + s * dil
                    x_ref[(l + 1) % 2, group, start : start + size, :] = x
                    activate(l + 1, group, x, start)
                    mirror(l + 1, group)
            elif e % 2 == 0:
                even = new
            else:
                for s in range(2):
                    col = (stretch * 2 * j + e - 1 + s * dil) * ch
                    value = pick(even[s], pltpu.roll(new[s], ch, 1))
                    made_ref[:, col : col + wide] = value.astype(made_ref.dtype)
                    col += stretch * ch
                    value = pick(pltpu.roll(even[s], ch, 1), new[s])
                    made_ref[:, col : col + wide] = value.astype(made_ref.dtype)
                if e == dil - 1:
                    send(j).start()

    unfinished = None
    for l in range(layers):
        dil = 2**l
        start = (edge - halos[l + 1]) // 8 * 8
        size = rows - 2 * start
        count = (tile + 2 * halos[l + 1]) // (4 * dil)
        blocks = [(j, e) for j in reversed(range(count)) for e in range(dil)]
        for at in range(0, len(blocks), GROUP):
            some = blocks[at : at + GROUP]
            need = [(2 * j + s) * dil + e for j, e in some for s in range(3)]
            if l == 0:
                for group in need:
                    if group not in ready[0]:
                        begin(group)
            if not ready[l].issuperset(need):
                finish(*unfinished)
                unfinished = None
            assert ready[l].issuperset(need)

            def taps(j, e):
                return [
                    g_ref[(2 * j + s) * dil + e, BASE + start + i * dil : BASE + start + i * dil + size, :].astype(
                        jnp.bfloat16
                    )
                    for i in (-1, 0, 1)
                    for s in range(3)
                ]

            lhs = jnp.concatenate([jnp.concatenate(taps(j, e), axis=1) for j, e in some], axis=0)
            acc = jnp.dot(lhs, t_refs[l][...], preferred_element_type=jnp.float32)
            if unfinished:
                finish(*unfinished)
            unfinished = (l, some, acc)
    finish(*unfinished)
    for j in range(tile // (2 * stretch)):
        send(j).wait()


def tile_call(npos, noff, order, layers, block_slot, table, proj_weight, proj_bias, conv_bias, banded):
    tile = table.shape[1]
    ch = proj_weight.shape[0] // 2
    vmem = pl.BlockSpec(memory_space=pltpu.VMEM)
    wide = 2 * ch
    groups = tile // 2 + 2**layers - 1
    high = tile + 2 * EDGE
    return pl.pallas_call(
        functools.partial(tile_kernel, (layers, tile, ch, npos, noff, order)),
        out_shape=jax.ShapeDtypeStruct((tile, tile * ch), jnp.bfloat16),
        in_specs=[pl.BlockSpec(memory_space=pltpu.SMEM)]
        + [vmem] * (4 + layers),
        out_specs=pl.BlockSpec(memory_space=pl.ANY),
        scratch_shapes=[
            pltpu.VMEM((2, groups, high, wide), jnp.float32),
            pltpu.VMEM((groups, high + 2 * BASE, wide), jnp.float32),
            pltpu.VMEM(((EDGE + 1) * (EDGE + tile), wide), jnp.float32),
            pltpu.VMEM(((tile + 1) * EDGE, wide), jnp.float32),
            pltpu.VMEM(((EDGE + 1) * EDGE, wide), jnp.float32),
            pltpu.VMEM((high, wide), jnp.float32),
            pltpu.VMEM((tile, tile * ch), jnp.bfloat16),
            pltpu.SemaphoreType.DMA((tile // 2 ** (layers + 1),)),
        ],
        compiler_params=pltpu.CompilerParams(vmem_limit_bytes=48 * 1024 * 1024),
        cost_estimate=pl.CostEstimate(flops=8000000000, bytes_accessed=4000000, transcendentals=2000000),
    )(block_slot, table, proj_weight, proj_bias, conv_bias, *banded)


def parameters_kernel(
    slot_ref, emb_ref, pw_ref, pb_ref, cb_ref, cw_ref, slot2_ref, own_ref, pw2_ref, pb2_ref, cb2_ref, cw2_ref
):
    for b in range(slot_ref.shape[0]):
        slot2_ref[b] = slot_ref[b]
    own_ref[0] = emb_ref[...]
    cw2_ref[...] = cw_ref[...]
    for ref, to, axis in ((pw_ref, pw2_ref, 0), (pb_ref, pb2_ref, 1), (cb_ref, cb2_ref, 1)):
        to[...] = jnp.concatenate([ref[...]] * 2, axis=axis)


def parameters_call(block_slot, bin_embed, proj_weight, proj_bias, conv_bias, weights):
    vmem, smem = pl.BlockSpec(memory_space=pltpu.VMEM), pl.BlockSpec(memory_space=pltpu.SMEM)
    ch, emb = proj_weight.shape
    return pl.pallas_call(
        parameters_kernel,
        out_shape=(
            pltpu.SMEM(block_slot.shape, block_slot.dtype),
            pltpu.VMEM((1,) + bin_embed.shape, bin_embed.dtype),
            pltpu.VMEM((2 * ch, emb), proj_weight.dtype),
            pltpu.VMEM((1, 2 * ch), proj_bias.dtype),
            pltpu.VMEM((conv_bias.shape[0], 2 * ch), conv_bias.dtype),
            pltpu.VMEM(weights.shape, weights.dtype),
        ),
        in_specs=[smem] + [vmem] * 5,
        out_specs=(smem,) + (vmem,) * 5,
        cost_estimate=pl.CostEstimate(flops=1000000, bytes_accessed=1000000, transcendentals=0),
    )(block_slot, bin_embed, proj_weight, proj_bias, conv_bias, weights)


def band_call(weights, which):
    layers, ch, taps = weights.shape
    weights = pltpu.with_memory_space_constraint(weights, pltpu.VMEM)
    vmem = pl.BlockSpec(memory_space=pltpu.VMEM)
    return pl.pallas_call(
        functools.partial(weights_kernel, ch, which),
        out_shape=(pltpu.VMEM((2 * taps, 4 * ch), weights.dtype),) * len(which),
        in_specs=[vmem],
        out_specs=(vmem,) * len(which),
        cost_estimate=pl.CostEstimate(flops=1000000, bytes_accessed=1000000, transcendentals=0),
    )(weights)


def on_device(bin_embed, block_slot, proj_weight, proj_bias, conv_weight, conv_bias):
    npos, noff = lax.axis_size("pos"), lax.axis_size("off")
    tile, emb = bin_embed.shape
    layers, taps, ch = conv_weight.shape
    order = tuple(reversed(range(npos.bit_length() - 1))) if npos & (npos - 1) == 0 else ()
    turned = jnp.swapaxes(conv_weight, 1, 2)
    table = bin_embed[None]
    banded, todo = [], tuple(range(layers))
    small = (block_slot, bin_embed, proj_weight.T, proj_bias[None], conv_bias, turned)
    for stage, bit in enumerate(order):
        there = lax.ppermute(table, "pos", [(i, i ^ (1 << bit | 1)) for i in range(npos)])
        if stage == 0:
            slots, table, *small, turned = parameters_call(*small)
            there, table, small, slots, turned = lax.optimization_barrier((there, table, small, slots, turned))
        elif todo:
            made = band_call(turned, todo[:2])
            there, made, turned = lax.optimization_barrier((there, made, turned))
            banded, todo = banded + list(made), todo[2:]
        table = jnp.concatenate([table, there], axis=0)
    if not order:
        slots, _, *small, turned = parameters_call(*small)
        table = lax.all_gather(bin_embed, "pos")
    if todo:
        banded += band_call(turned, todo)
    out = tile_call(npos, noff, order, layers, slots, table, *small, banded)
    return out.reshape(1, 1, tile, tile * ch)


def solution(mesh):
    placed = (P("pos", None), P(), P(), P(), P(), P())
    return jax.shard_map(
        on_device,
        mesh=mesh,
        in_specs=placed,
        out_specs=P("pos", "off", None, None),
        check_vma=False,
    )
```

```python
import functools

import jax
import jax.numpy as jnp
from jax import lax
from jax.experimental import pallas as pl
from jax.experimental.pallas import tpu as pltpu
from jax.sharding import PartitionSpec as P

GROUP = 4
BASE = 8
EDGE = 16


def gelu(x):
    u = x * (0.7978845608028654 + 0.035677408136300125 * (x * x))
    half = 0.5 * x
    return half + half * jnp.tanh(u)


def place(col, halo, dil):
    u = col + halo
    within = u % (2 * dil)
    return (u // (2 * dil)) * dil + within % dil, within // dil


def columns(group, halo, dil):
    first = (group // dil) * 2 * dil + group % dil - halo
    return first, first + dil


def weights_kernel(ch, which, cw_ref, *t_refs):
    zero = jnp.zeros((ch, ch), cw_ref.dtype)
    for l, t_ref in zip(which, t_refs):
        taps = jnp.transpose(cw_ref[l].astype(jnp.float32)).astype(t_ref.dtype)
        for i in range(3):
            for a in range(6):
                row = [
                    taps[(3 * i + a - b) * ch : (3 * i + a - b + 1) * ch] if 0 <= a - b <= 2 else zero
                    for b in (0, 2, 1, 3)
                ]
                t_ref[(6 * i + a) * ch : (6 * i + a + 1) * ch, :] = jnp.concatenate(row, axis=1)


def tile_kernel(dims, slot_ref, bin_ref, pb_ref, cb_ref, *refs):
    layers, tile, ch, npos, noff, order = dims
    t_refs = refs[:layers]
    out_ref, x_ref, g_ref, side_ref, left_ref, corner_ref, bins_ref, made_ref, sems = refs[layers:]
    wide = 2 * ch
    edge = EDGE
    rows = tile + 2 * edge
    halos = [2**layers - 2**l for l in range(layers + 1)]
    top, mid, bot = BASE, BASE + edge, BASE + edge + tile
    side_step, left_step = edge + 1, tile + 1
    me, off = lax.axis_index("pos"), lax.axis_index("off")
    low = lax.broadcasted_iota(jnp.int32, (1, wide), 1) < ch
    diagonal, beside = off == 0, off == 1

    def pick(lo, hi):
        return jnp.where(low, lo, hi)

    def both(value):
        turned = pltpu.roll(value, ch, 1)
        return pick(value, turned), pick(turned, value)

    def block(b):
        slot = slot_ref[lax.rem(b + npos, npos)]
        if not order:
            return slot
        away = jnp.bitwise_xor(slot, me)
        bits = [jnp.bitwise_and(lax.shift_right_logical(away, bit), 1) for bit in order]
        for bit in bits[:-1]:
            bits[-1] = jnp.bitwise_xor(bits[-1], bit)
        return sum(bit << n for n, bit in enumerate(bits))

    def bins(b):
        first, here, last = (both(bin_ref[block(b + k)].astype(jnp.float32)) for k in (-1, 0, 1))
        return jnp.concatenate([first[1][tile // 2 - edge :], here[0], here[1], last[0][:edge]], axis=0)

    row_bins = bins(me) + pb_ref[...]
    bins_ref[...] = bins(me + off)
    pairs = (tile + 2 * halos[0]) // 2
    first = edge - halos[0]
    col_bins = pick(
        bins_ref[pl.ds(first, pairs, stride=2), :], bins_ref[pl.ds(first + 1, pairs, stride=2), :]
    )

    keeps = {
        (a, b): (jnp.abs(off + b - a) < noff).astype(jnp.float32) for a in (-1, 0, 1) for b in (-1, 0, 1)
    }

    def band(col):
        return -1 if col < 0 else 1 if col >= tile else 0

    ready = [set() for _ in range(layers)]
    seen = [set() for _ in range(layers)]
    waiting = [[] for _ in range(layers)]

    def activate(l, group, x, start):
        lo, hi = (band(c) for c in columns(group, halos[l], 2**l))
        size = x.shape[0]
        for a, begin, end in ((-1, 0, edge), (0, edge, edge + tile), (1, edge + tile, rows)):
            begin, end = max(begin, start), min(end, start + size)
            if begin < end:
                g = gelu(x[begin - start : end - start].astype(jnp.bfloat16)).astype(jnp.float32)
                if (a, lo, hi) != (0, 0, 0):
                    g = g * pick(keeps[a, lo], keeps[a, hi])
                g_ref[group, BASE + begin : BASE + end, :] = g

    def mirror(l, group):
        halo, dil = halos[l], 2**l
        deep = -(-halo // 8) * 8
        cols = columns(group, halo, dil)
        seen[l].update(cols)
        if any(tile <= c < tile + halo for c in cols):
            for c, value in zip(cols, both(g_ref[group, top:bot, :])):
                if c >= tile:
                    side_ref[pl.ds(c - tile, edge + tile, stride=side_step), :] = value
        if any(0 <= c < tile for c in cols):
            for c, value in zip(cols, both(g_ref[group, top:mid, :])):
                if 0 <= c < tile:
                    left_ref[pl.ds(c, edge, stride=left_step), :] = value
        if any(0 <= c < halo for c in cols):
            for c, value in zip(cols, both(g_ref[group, bot - edge : bot, :])):
                if 0 <= c < halo:
                    corner_ref[pl.ds(c, edge, stride=side_step), :] = value
        waiting[l].append(group)
        for group in list(waiting[l]):
            c1, c2 = columns(group, halo, dil)
            if c1 < tile and not seen[l].issuperset(range(tile, tile + halo)):
                continue
            if c1 < 0 and not seen[l].issuperset(range(tile)):
                continue
            waiting[l].remove(group)
            ready[l].add(group)
            if c1 < tile:
                now = g_ref[group, bot : bot + deep, :]
                at = [(c + edge) * side_step for c in (c1, c2)]
                made = [side_ref[k : k + deep, :] if c < tile else now for c, k in zip((c1, c2), at)]
                new = jnp.where(diagonal, pick(*made), now)
                if c1 < 0:
                    made = [corner_ref[k : k + deep, :] if c < 0 else now for c, k in zip((c1, c2), at)]
                    new = jnp.where(beside, pick(*made), new)
                g_ref[group, bot : bot + deep, :] = new
            if c1 < 0:
                now = g_ref[group, mid:bot, :]
                at = [(c + edge) * left_step for c in (c1, c2)]
                made = [left_ref[k : k + tile, :] if c < 0 else now for c, k in zip((c1, c2), at)]
                g_ref[group, mid:bot, :] = jnp.where(diagonal, pick(*made), now)

    def begin(group):
        x = row_bins + col_bins[group : group + 1]
        x_ref[0, group, :, :] = x
        activate(0, group, x, 0)
        ready[0].add(group)

    stretch = 2**layers
    span = 2 * stretch * ch

    def send(j):
        here = (slice(None), pl.ds(j * span, span))
        return pltpu.make_async_copy(made_ref.at[here], out_ref.at[here], sems.at[j])

    def finish(l, some, acc):
        dil = 2**l
        start = (edge - halos[l + 1]) // 8 * 8
        size = rows - 2 * start
        for n, (j, e) in enumerate(some):
            old = [x_ref[l % 2, (2 * j + s) * dil + e, start : start + size, :] for s in range(3)]
            carried = (pick(pltpu.roll(old[0], ch, 1), old[1]), pick(old[1], pltpu.roll(old[2], ch, 1)))
            new = [
                acc[n * size : (n + 1) * size, s * wide : (s + 1) * wide] + carried[s] + cb_ref[l : l + 1, :]
                for s in range(2)
            ]
            if l + 1 < layers:
                for s, x in enumerate(new):
                    group = j * 2 * dil + e + s * dil
                    x_ref[(l + 1) % 2, group, start : start + size, :] = x
                    activate(l + 1, group, x, start)
                    mirror(l + 1, group)
            elif e % 2 == 0:
                even = new
            else:
                for s in range(2):
                    col = (stretch * 2 * j + e - 1 + s * dil) * ch
                    value = pick(even[s], pltpu.roll(new[s], ch, 1))
                    made_ref[:, col : col + wide] = value.astype(made_ref.dtype)
                    col += stretch * ch
                    value = pick(pltpu.roll(even[s], ch, 1), new[s])
                    made_ref[:, col : col + wide] = value.astype(made_ref.dtype)
                if e == dil - 1:
                    send(j).start()

    unfinished = None
    for l in range(layers):
        dil = 2**l
        start = (edge - halos[l + 1]) // 8 * 8
        size = rows - 2 * start
        count = (tile + 2 * halos[l + 1]) // (4 * dil)
        blocks = [(j, e) for j in reversed(range(count)) for e in range(dil)]
        for at in range(0, len(blocks), GROUP):
            some = blocks[at : at + GROUP]
            need = [(2 * j + s) * dil + e for j, e in some for s in range(3)]
            if l == 0:
                for group in need:
                    if group not in ready[0]:
                        begin(group)
            if not ready[l].issuperset(need):
                finish(*unfinished)
                unfinished = None
            assert ready[l].issuperset(need)

            def taps(j, e):
                return [
                    g_ref[(2 * j + s) * dil + e, BASE + start + i * dil : BASE + start + i * dil + size, :].astype(
                        jnp.bfloat16
                    )
                    for i in (-1, 0, 1)
                    for s in range(3)
                ]

            lhs = jnp.concatenate([jnp.concatenate(taps(j, e), axis=1) for j, e in some], axis=0)
            acc = jnp.dot(lhs, t_refs[l][...], preferred_element_type=jnp.float32)
            if unfinished:
                finish(*unfinished)
            unfinished = (l, some, acc)
    finish(*unfinished)
    for j in range(tile // (2 * stretch)):
        send(j).wait()


def tile_call(npos, noff, order, layers, block_slot, table, proj_bias, conv_bias, banded):
    tile = 2 * table.shape[1]
    ch = proj_bias.shape[1] // 2
    vmem = pl.BlockSpec(memory_space=pltpu.VMEM)
    wide = 2 * ch
    groups = tile // 2 + 2**layers - 1
    high = tile + 2 * EDGE
    return pl.pallas_call(
        functools.partial(tile_kernel, (layers, tile, ch, npos, noff, order)),
        out_shape=jax.ShapeDtypeStruct((tile, tile * ch), jnp.bfloat16),
        in_specs=[pl.BlockSpec(memory_space=pltpu.SMEM)]
        + [vmem] * (3 + layers),
        out_specs=pl.BlockSpec(memory_space=pl.ANY),
        scratch_shapes=[
            pltpu.VMEM((2, groups, high, wide), jnp.float32),
            pltpu.VMEM((groups, high + 2 * BASE, wide), jnp.float32),
            pltpu.VMEM(((EDGE + 1) * (EDGE + tile), wide), jnp.float32),
            pltpu.VMEM(((tile + 1) * EDGE, wide), jnp.float32),
            pltpu.VMEM(((EDGE + 1) * EDGE, wide), jnp.float32),
            pltpu.VMEM((high, wide), jnp.float32),
            pltpu.VMEM((tile, tile * ch), jnp.bfloat16),
            pltpu.SemaphoreType.DMA((tile // 2 ** (layers + 1),)),
        ],
        compiler_params=pltpu.CompilerParams(vmem_limit_bytes=48 * 1024 * 1024),
        cost_estimate=pl.CostEstimate(flops=8000000000, bytes_accessed=4000000, transcendentals=2000000),
    )(block_slot, table, proj_bias, conv_bias, *banded)


def project(emb, weight):
    made = lax.dot_general(emb, weight, (((1,), (1,)), ((), ())), preferred_element_type=jnp.float32)
    half = made.shape[0] // 2
    return jnp.concatenate([made[:half], made[half:]], axis=1).astype(jnp.bfloat16)


def parameters_kernel(
    slot_ref, emb_ref, pw_ref, pb_ref, cb_ref, cw_ref, slot2_ref, own_ref, pw2_ref, pb2_ref, cb2_ref, cw2_ref
):
    for b in range(slot_ref.shape[0]):
        slot2_ref[b] = slot_ref[b]
    own_ref[0] = project(emb_ref[...], pw_ref[...])
    pw2_ref[...] = pw_ref[...]
    cw2_ref[...] = cw_ref[...]
    for ref, to in ((pb_ref, pb2_ref), (cb_ref, cb2_ref)):
        to[...] = jnp.concatenate([ref[...]] * 2, axis=1)


def parameters_call(block_slot, bin_embed, proj_weight, proj_bias, conv_bias, weights):
    vmem, smem = pl.BlockSpec(memory_space=pltpu.VMEM), pl.BlockSpec(memory_space=pltpu.SMEM)
    tile, ch = bin_embed.shape[0], proj_weight.shape[0]
    return pl.pallas_call(
        parameters_kernel,
        out_shape=(
            pltpu.SMEM(block_slot.shape, block_slot.dtype),
            pltpu.VMEM((1, tile // 2, 2 * ch), jnp.bfloat16),
            pltpu.VMEM(proj_weight.shape, proj_weight.dtype),
            pltpu.VMEM((1, 2 * ch), proj_bias.dtype),
            pltpu.VMEM((conv_bias.shape[0], 2 * ch), conv_bias.dtype),
            pltpu.VMEM(weights.shape, weights.dtype),
        ),
        in_specs=[smem] + [vmem] * 5,
        out_specs=(smem,) + (vmem,) * 5,
        cost_estimate=pl.CostEstimate(flops=1000000, bytes_accessed=1000000, transcendentals=0),
    )(block_slot, bin_embed, proj_weight, proj_bias, conv_bias, weights)


def project_kernel(own_ref, emb_ref, pw_ref, out_ref):
    count = emb_ref.shape[0]
    if own_ref is not None:
        out_ref[0] = own_ref[0]
    for b in range(count):
        out_ref[out_ref.shape[0] - count + b] = project(emb_ref[b], pw_ref[...])


def project_call(own, embeds, proj_weight):
    vmem = pl.BlockSpec(memory_space=pltpu.VMEM)
    blocks, tile, _ = embeds.shape
    ch = proj_weight.shape[0]
    kernel, args = project_kernel, (own, embeds, proj_weight)
    if own is None:
        kernel, args = functools.partial(project_kernel, None), args[1:]
    args = [pltpu.with_memory_space_constraint(arg, pltpu.VMEM) for arg in args]
    return pl.pallas_call(
        kernel,
        out_shape=pltpu.VMEM((blocks + len(args) - 2, tile // 2, 2 * ch), jnp.bfloat16),
        in_specs=[vmem] * len(args),
        out_specs=vmem,
        cost_estimate=pl.CostEstimate(flops=1000000, bytes_accessed=100000, transcendentals=0),
    )(*args)


def band_call(weights, which):
    layers, ch, taps = weights.shape
    weights = pltpu.with_memory_space_constraint(weights, pltpu.VMEM)
    vmem = pl.BlockSpec(memory_space=pltpu.VMEM)
    return pl.pallas_call(
        functools.partial(weights_kernel, ch, which),
        out_shape=(pltpu.VMEM((2 * taps, 4 * ch), weights.dtype),) * len(which),
        in_specs=[vmem],
        out_specs=(vmem,) * len(which),
        cost_estimate=pl.CostEstimate(flops=1000000, bytes_accessed=1000000, transcendentals=0),
    )(weights)


def on_device(bin_embed, block_slot, proj_weight, proj_bias, conv_weight, conv_bias):
    npos, noff = lax.axis_size("pos"), lax.axis_size("off")
    tile, emb = bin_embed.shape
    layers, taps, ch = conv_weight.shape
    order = tuple(reversed(range(npos.bit_length() - 1))) if npos & (npos - 1) == 0 else ()
    turned = jnp.swapaxes(conv_weight, 1, 2)
    table = bin_embed[None]
    banded, todo = [], tuple(range(layers))
    small = (block_slot, bin_embed, proj_weight.T, proj_bias[None], conv_bias, turned)
    for stage, bit in enumerate(order):
        there = lax.ppermute(table, "pos", [(i, i ^ (1 << bit | 1)) for i in range(npos)])
        if stage == 0:
            slots, table, projection, *small, turned = parameters_call(*small)
            there, table, small, slots, turned = lax.optimization_barrier((there, table, small, slots, turned))
            table = project_call(table, there, projection)
            continue
        if todo:
            made = band_call(turned, todo[:2])
            there, made, turned = lax.optimization_barrier((there, made, turned))
            banded, todo = banded + list(made), todo[2:]
        table = jnp.concatenate([table, there], axis=0)
    if not order:
        slots, _, projection, *small, turned = parameters_call(*small)
        table = project_call(None, lax.all_gather(bin_embed, "pos"), projection)
    if todo:
        banded += band_call(turned, todo)
    out = tile_call(npos, noff, order, layers, slots, table, *small, banded)
    return out.reshape(1, 1, tile, tile * ch)


def solution(mesh):
    placed = (P("pos", None), P(), P(), P(), P(), P())
    return jax.shard_map(
        on_device,
        mesh=mesh,
        in_specs=placed,
        out_specs=P("pos", "off", None, None),
        check_vma=False,
    )
```

```python
import functools

import jax
import jax.numpy as jnp
from jax import lax
from jax.experimental import pallas as pl
from jax.experimental.pallas import tpu as pltpu
from jax.sharding import PartitionSpec as P

GROUP = 4
FIRST_GROUP = 6
BASE = 8
EDGE = 16


def gelu(x):
    u = x * (0.7978845608028654 + 0.035677408136300125 * (x * x))
    half = 0.5 * x
    return half + half * jnp.tanh(u)


def place(col, halo, dil):
    u = col + halo
    within = u % (2 * dil)
    return (u // (2 * dil)) * dil + within % dil, within // dil


def columns(group, halo, dil):
    first = (group // dil) * 2 * dil + group % dil - halo
    return first, first + dil


def weights_kernel(ch, which, cw_ref, *t_refs):
    zero = jnp.zeros((ch, ch), cw_ref.dtype)
    for l, t_ref in zip(which, t_refs):
        taps = jnp.transpose(cw_ref[l].astype(jnp.float32)).astype(t_ref.dtype)
        for i in range(3):
            for a in range(6):
                row = [
                    taps[(3 * i + a - b) * ch : (3 * i + a - b + 1) * ch] if 0 <= a - b <= 2 else zero
                    for b in (0, 2, 1, 3)
                ]
                t_ref[(6 * i + a) * ch : (6 * i + a + 1) * ch, :] = jnp.concatenate(row, axis=1)


def tile_kernel(dims, slot_ref, bin_ref, pb_ref, cb_ref, *refs):
    layers, tile, ch, npos, noff, order = dims
    t_refs = refs[:layers]
    out_ref, x_ref, g_ref, side_ref, left_ref, corner_ref, bins_ref, made_ref, sems = refs[layers:]
    wide = 2 * ch
    edge = EDGE
    rows = tile + 2 * edge
    halos = [2**layers - 2**l for l in range(layers + 1)]
    top, mid, bot = BASE, BASE + edge, BASE + edge + tile
    side_step, left_step = edge + 1, tile + 1
    me, off = lax.axis_index("pos"), lax.axis_index("off")
    low = lax.broadcasted_iota(jnp.int32, (1, wide), 1) < ch
    diagonal, beside = off == 0, off == 1

    def pick(lo, hi):
        return jnp.where(low, lo, hi)

    def both(value):
        turned = pltpu.roll(value, ch, 1)
        return pick(value, turned), pick(turned, value)

    def block(b):
        slot = slot_ref[lax.rem(b + npos, npos)]
        if not order:
            return slot
        away = jnp.bitwise_xor(slot, me)
        bits = [jnp.bitwise_and(lax.shift_right_logical(away, bit), 1) for bit in order]
        for bit in bits[:-1]:
            bits[-1] = jnp.bitwise_xor(bits[-1], bit)
        return sum(bit << n for n, bit in enumerate(bits))

    def bins(b):
        first, here, last = (both(bin_ref[block(b + k)].astype(jnp.float32)) for k in (-1, 0, 1))
        return jnp.concatenate([first[1][tile // 2 - edge :], here[0], here[1], last[0][:edge]], axis=0)

    row_bins = bins(me) + pb_ref[...]
    bins_ref[...] = bins(me + off)
    pairs = (tile + 2 * halos[0]) // 2
    first = edge - halos[0]
    col_bins = pick(
        bins_ref[pl.ds(first, pairs, stride=2), :], bins_ref[pl.ds(first + 1, pairs, stride=2), :]
    )

    keeps = {
        (a, b): (jnp.abs(off + b - a) < noff).astype(jnp.float32) for a in (-1, 0, 1) for b in (-1, 0, 1)
    }

    def band(col):
        return -1 if col < 0 else 1 if col >= tile else 0

    ready = [set() for _ in range(layers)]
    seen = [set() for _ in range(layers)]
    waiting = [[] for _ in range(layers)]

    def activate(l, group, x, start):
        lo, hi = (band(c) for c in columns(group, halos[l], 2**l))
        size = x.shape[0]
        for a, begin, end in ((-1, 0, edge), (0, edge, edge + tile), (1, edge + tile, rows)):
            begin, end = max(begin, start), min(end, start + size)
            if begin < end:
                g = gelu(x[begin - start : end - start].astype(jnp.bfloat16)).astype(jnp.float32)
                if (a, lo, hi) != (0, 0, 0):
                    g = g * pick(keeps[a, lo], keeps[a, hi])
                g_ref[group, BASE + begin : BASE + end, :] = g

    def mirror(l, group):
        halo, dil = halos[l], 2**l
        deep = -(-halo // 8) * 8
        cols = columns(group, halo, dil)
        seen[l].update(cols)
        if any(tile <= c < tile + halo for c in cols):
            for c, value in zip(cols, both(g_ref[group, top:bot, :])):
                if c >= tile:
                    side_ref[pl.ds(c - tile, edge + tile, stride=side_step), :] = value
        if any(0 <= c < tile for c in cols):
            for c, value in zip(cols, both(g_ref[group, top:mid, :])):
                if 0 <= c < tile:
                    left_ref[pl.ds(c, edge, stride=left_step), :] = value
        if any(0 <= c < halo for c in cols):
            for c, value in zip(cols, both(g_ref[group, bot - edge : bot, :])):
                if 0 <= c < halo:
                    corner_ref[pl.ds(c, edge, stride=side_step), :] = value
        waiting[l].append(group)
        for group in list(waiting[l]):
            c1, c2 = columns(group, halo, dil)
            if c1 < tile and not seen[l].issuperset(range(tile, tile + halo)):
                continue
            if c1 < 0 and not seen[l].issuperset(range(tile)):
                continue
            waiting[l].remove(group)
            ready[l].add(group)
            if c1 < tile:
                now = g_ref[group, bot : bot + deep, :]
                at = [(c + edge) * side_step for c in (c1, c2)]
                made = [side_ref[k : k + deep, :] if c < tile else now for c, k in zip((c1, c2), at)]
                new = jnp.where(diagonal, pick(*made), now)
                if c1 < 0:
                    made = [corner_ref[k : k + deep, :] if c < 0 else now for c, k in zip((c1, c2), at)]
                    new = jnp.where(beside, pick(*made), new)
                g_ref[group, bot : bot + deep, :] = new
            if c1 < 0:
                now = g_ref[group, mid:bot, :]
                at = [(c + edge) * left_step for c in (c1, c2)]
                made = [left_ref[k : k + tile, :] if c < 0 else now for c, k in zip((c1, c2), at)]
                g_ref[group, mid:bot, :] = jnp.where(diagonal, pick(*made), now)

    def begin(group):
        x = row_bins + col_bins[group : group + 1]
        x_ref[0, group, :, :] = x
        activate(0, group, x, 0)
        ready[0].add(group)

    stretch = 2**layers
    span = 2 * stretch * ch

    def send(j):
        here = (slice(None), pl.ds(j * span, span))
        return pltpu.make_async_copy(made_ref.at[here], out_ref.at[here], sems.at[j])

    def finish(l, some, acc):
        dil = 2**l
        start = (edge - halos[l + 1]) // 8 * 8
        size = rows - 2 * start
        for n, (j, e) in enumerate(some):
            old = [x_ref[l % 2, (2 * j + s) * dil + e, start : start + size, :] for s in range(3)]
            carried = (pick(pltpu.roll(old[0], ch, 1), old[1]), pick(old[1], pltpu.roll(old[2], ch, 1)))
            new = [
                acc[n * size : (n + 1) * size, s * wide : (s + 1) * wide] + carried[s] + cb_ref[l : l + 1, :]
                for s in range(2)
            ]
            if l + 1 < layers:
                for s, x in enumerate(new):
                    group = j * 2 * dil + e + s * dil
                    x_ref[(l + 1) % 2, group, start : start + size, :] = x
                    activate(l + 1, group, x, start)
                    mirror(l + 1, group)
            elif e % 2 == 0:
                even = new
            else:
                for s in range(2):
                    col = (stretch * 2 * j + e - 1 + s * dil) * ch
                    value = pick(even[s], pltpu.roll(new[s], ch, 1))
                    made_ref[:, col : col + wide] = value.astype(made_ref.dtype)
                    col += stretch * ch
                    value = pick(pltpu.roll(even[s], ch, 1), new[s])
                    made_ref[:, col : col + wide] = value.astype(made_ref.dtype)
                if e == dil - 1:
                    send(j).start()

    unfinished = None
    for l in range(layers):
        dil = 2**l
        start = (edge - halos[l + 1]) // 8 * 8
        size = rows - 2 * start
        count = (tile + 2 * halos[l + 1]) // (4 * dil)
        blocks = [(j, e) for j in reversed(range(count)) for e in range(dil)]
        group_size = GROUP if l else FIRST_GROUP
        for at in range(0, len(blocks), group_size):
            some = blocks[at : at + group_size]
            need = [(2 * j + s) * dil + e for j, e in some for s in range(3)]
            if l == 0:
                for group in need:
                    if group not in ready[0]:
                        begin(group)
            if not ready[l].issuperset(need):
                finish(*unfinished)
                unfinished = None
            assert ready[l].issuperset(need)

            def taps(j, e):
                return [
                    g_ref[(2 * j + s) * dil + e, BASE + start + i * dil : BASE + start + i * dil + size, :].astype(
                        jnp.bfloat16
                    )
                    for i in (-1, 0, 1)
                    for s in range(3)
                ]

            lhs = jnp.concatenate([jnp.concatenate(taps(j, e), axis=1) for j, e in some], axis=0)
            acc = jnp.dot(lhs, t_refs[l][...], preferred_element_type=jnp.float32)
            if unfinished:
                finish(*unfinished)
            unfinished = (l, some, acc)
    finish(*unfinished)
    for j in range(tile // (2 * stretch)):
        send(j).wait()


def tile_call(npos, noff, order, layers, block_slot, table, proj_bias, conv_bias, banded):
    tile = 2 * table.shape[1]
    ch = proj_bias.shape[1] // 2
    vmem = pl.BlockSpec(memory_space=pltpu.VMEM)
    wide = 2 * ch
    groups = tile // 2 + 2**layers - 1
    high = tile + 2 * EDGE
    return pl.pallas_call(
        functools.partial(tile_kernel, (layers, tile, ch, npos, noff, order)),
        out_shape=jax.ShapeDtypeStruct((tile, tile * ch), jnp.bfloat16),
        in_specs=[pl.BlockSpec(memory_space=pltpu.SMEM)]
        + [vmem] * (3 + layers),
        out_specs=pl.BlockSpec(memory_space=pl.ANY),
        scratch_shapes=[
            pltpu.VMEM((2, groups, high, wide), jnp.float32),
            pltpu.VMEM((groups, high + 2 * BASE, wide), jnp.float32),
            pltpu.VMEM(((EDGE + 1) * (EDGE + tile), wide), jnp.float32),
            pltpu.VMEM(((tile + 1) * EDGE, wide), jnp.float32),
            pltpu.VMEM(((EDGE + 1) * EDGE, wide), jnp.float32),
            pltpu.VMEM((high, wide), jnp.float32),
            pltpu.VMEM((tile, tile * ch), jnp.bfloat16),
            pltpu.SemaphoreType.DMA((tile // 2 ** (layers + 1),)),
        ],
        compiler_params=pltpu.CompilerParams(vmem_limit_bytes=48 * 1024 * 1024),
        cost_estimate=pl.CostEstimate(flops=8000000000, bytes_accessed=4000000, transcendentals=2000000),
    )(block_slot, table, proj_bias, conv_bias, *banded)


def project(emb, weight):
    made = lax.dot_general(emb, weight, (((1,), (1,)), ((), ())), preferred_element_type=jnp.float32)
    half = made.shape[0] // 2
    return jnp.concatenate([made[:half], made[half:]], axis=1).astype(jnp.bfloat16)


def parameters_kernel(
    slot_ref, emb_ref, pw_ref, pb_ref, cb_ref, cw_ref, slot2_ref, own_ref, pw2_ref, pb2_ref, cb2_ref, cw2_ref
):
    for b in range(slot_ref.shape[0]):
        slot2_ref[b] = slot_ref[b]
    own_ref[0] = project(emb_ref[...], pw_ref[...])
    pw2_ref[...] = pw_ref[...]
    cw2_ref[...] = cw_ref[...]
    for ref, to in ((pb_ref, pb2_ref), (cb_ref, cb2_ref)):
        to[...] = jnp.concatenate([ref[...]] * 2, axis=1)


def parameters_call(block_slot, bin_embed, proj_weight, proj_bias, conv_bias, weights):
    vmem, smem = pl.BlockSpec(memory_space=pltpu.VMEM), pl.BlockSpec(memory_space=pltpu.SMEM)
    tile, ch = bin_embed.shape[0], proj_weight.shape[0]
    return pl.pallas_call(
        parameters_kernel,
        out_shape=(
            pltpu.SMEM(block_slot.shape, block_slot.dtype),
            pltpu.VMEM((1, tile // 2, 2 * ch), jnp.bfloat16),
            pltpu.VMEM(proj_weight.shape, proj_weight.dtype),
            pltpu.VMEM((1, 2 * ch), proj_bias.dtype),
            pltpu.VMEM((conv_bias.shape[0], 2 * ch), conv_bias.dtype),
            pltpu.VMEM(weights.shape, weights.dtype),
        ),
        in_specs=[smem] + [vmem] * 5,
        out_specs=(smem,) + (vmem,) * 5,
        cost_estimate=pl.CostEstimate(flops=1000000, bytes_accessed=1000000, transcendentals=0),
    )(block_slot, bin_embed, proj_weight, proj_bias, conv_bias, weights)


def project_kernel(own_ref, emb_ref, pw_ref, out_ref):
    count = emb_ref.shape[0]
    if own_ref is not None:
        out_ref[0] = own_ref[0]
    for b in range(count):
        out_ref[out_ref.shape[0] - count + b] = project(emb_ref[b], pw_ref[...])


def project_call(own, embeds, proj_weight):
    vmem = pl.BlockSpec(memory_space=pltpu.VMEM)
    blocks, tile, _ = embeds.shape
    ch = proj_weight.shape[0]
    kernel, args = project_kernel, (own, embeds, proj_weight)
    if own is None:
        kernel, args = functools.partial(project_kernel, None), args[1:]
    args = [pltpu.with_memory_space_constraint(arg, pltpu.VMEM) for arg in args]
    return pl.pallas_call(
        kernel,
        out_shape=pltpu.VMEM((blocks + len(args) - 2, tile // 2, 2 * ch), jnp.bfloat16),
        in_specs=[vmem] * len(args),
        out_specs=vmem,
        cost_estimate=pl.CostEstimate(flops=1000000, bytes_accessed=100000, transcendentals=0),
    )(*args)


def band_call(weights, which):
    layers, ch, taps = weights.shape
    weights = pltpu.with_memory_space_constraint(weights, pltpu.VMEM)
    vmem = pl.BlockSpec(memory_space=pltpu.VMEM)
    return pl.pallas_call(
        functools.partial(weights_kernel, ch, which),
        out_shape=(pltpu.VMEM((2 * taps, 4 * ch), weights.dtype),) * len(which),
        in_specs=[vmem],
        out_specs=(vmem,) * len(which),
        cost_estimate=pl.CostEstimate(flops=1000000, bytes_accessed=1000000, transcendentals=0),
    )(weights)


def on_device(bin_embed, block_slot, proj_weight, proj_bias, conv_weight, conv_bias):
    npos, noff = lax.axis_size("pos"), lax.axis_size("off")
    tile, emb = bin_embed.shape
    layers, taps, ch = conv_weight.shape
    order = tuple(reversed(range(npos.bit_length() - 1))) if npos & (npos - 1) == 0 else ()
    turned = jnp.swapaxes(conv_weight, 1, 2)
    table = bin_embed[None]
    banded, todo = [], tuple(range(layers))
    small = (block_slot, bin_embed, proj_weight.T, proj_bias[None], conv_bias, turned)
    for stage, bit in enumerate(order):
        there = lax.ppermute(table, "pos", [(i, i ^ (1 << bit | 1)) for i in range(npos)])
        if stage == 0:
            slots, table, projection, *small, turned = parameters_call(*small)
            there, table, small, slots, turned = lax.optimization_barrier((there, table, small, slots, turned))
            table = project_call(table, there, projection)
            continue
        if todo:
            made = band_call(turned, todo[:2])
            there, made, turned = lax.optimization_barrier((there, made, turned))
            banded, todo = banded + list(made), todo[2:]
        table = jnp.concatenate([table, there], axis=0)
    if not order:
        slots, _, projection, *small, turned = parameters_call(*small)
        table = project_call(None, lax.all_gather(bin_embed, "pos"), projection)
    if todo:
        banded += band_call(turned, todo)
    out = tile_call(npos, noff, order, layers, slots, table, *small, banded)
    return out.reshape(1, 1, tile, tile * ch)


def solution(mesh):
    placed = (P("pos", None), P(), P(), P(), P(), P())
    return jax.shard_map(
        on_device,
        mesh=mesh,
        in_specs=placed,
        out_specs=P("pos", "off", None, None),
        check_vma=False,
    )
```

```python
import functools

import jax
import jax.numpy as jnp
from jax import lax
from jax.experimental import pallas as pl
from jax.experimental.pallas import tpu as pltpu
from jax.sharding import PartitionSpec as P

GROUP = 4
FIRST_GROUP = 6
BASE = 8
EDGE = 16


def gelu(x):
    u = x * (0.7978845608028654 + 0.035677408136300125 * (x * x))
    half = 0.5 * x
    return half + half * jnp.tanh(u)


def place(col, halo, dil):
    u = col + halo
    within = u % (2 * dil)
    return (u // (2 * dil)) * dil + within % dil, within // dil


def columns(group, halo, dil):
    first = (group // dil) * 2 * dil + group % dil - halo
    return first, first + dil


def weights_kernel(ch, which, cw_ref, *t_refs):
    zero = jnp.zeros((ch, ch), cw_ref.dtype)
    for l, t_ref in zip(which, t_refs):
        taps = jnp.transpose(cw_ref[l].astype(jnp.float32)).astype(t_ref.dtype)
        for i in range(3):
            for a in range(6):
                row = [
                    taps[(3 * i + a - b) * ch : (3 * i + a - b + 1) * ch] if 0 <= a - b <= 2 else zero
                    for b in (0, 2, 1, 3)
                ]
                t_ref[(6 * i + a) * ch : (6 * i + a + 1) * ch, :] = jnp.concatenate(row, axis=1)


def tile_kernel(dims, slot_ref, bin_ref, pb_ref, cb_ref, *refs):
    layers, tile, ch, npos, noff, order = dims
    t_refs = refs[:layers]
    out_ref, x_ref, g_ref, side_ref, left_ref, corner_ref, bins_ref, made_ref, sems = refs[layers:]
    wide = 2 * ch
    edge = EDGE
    rows = tile + 2 * edge
    halos = [2**layers - 2**l for l in range(layers + 1)]
    top, mid, bot = BASE, BASE + edge, BASE + edge + tile
    side_step, left_step = edge + 1, tile + 1
    me, off = lax.axis_index("pos"), lax.axis_index("off")
    low = lax.broadcasted_iota(jnp.int32, (1, wide), 1) < ch
    diagonal, beside = off == 0, off == 1

    def pick(lo, hi):
        return jnp.where(low, lo, hi)

    def both(value):
        turned = pltpu.roll(value, ch, 1)
        return pick(value, turned), pick(turned, value)

    def block(b):
        slot = slot_ref[lax.rem(b + npos, npos)]
        if not order:
            return slot
        away = jnp.bitwise_xor(slot, me)
        bits = [jnp.bitwise_and(lax.shift_right_logical(away, bit), 1) for bit in order]
        for bit in bits[:-1]:
            bits[-1] = jnp.bitwise_xor(bits[-1], bit)
        return sum(bit << n for n, bit in enumerate(bits))

    def bins(b):
        first, here, last = (both(bin_ref[block(b + k)].astype(jnp.float32)) for k in (-1, 0, 1))
        return jnp.concatenate([first[1][tile // 2 - edge :], here[0], here[1], last[0][:edge]], axis=0)

    row_bins = bins(me) + pb_ref[...]
    bins_ref[...] = bins(me + off)
    pairs = (tile + 2 * halos[0]) // 2
    first = edge - halos[0]
    col_bins = pick(
        bins_ref[pl.ds(first, pairs, stride=2), :], bins_ref[pl.ds(first + 1, pairs, stride=2), :]
    )

    keeps = {
        (a, b): (jnp.abs(off + b - a) < noff).astype(jnp.float32) for a in (-1, 0, 1) for b in (-1, 0, 1)
    }

    def band(col):
        return -1 if col < 0 else 1 if col >= tile else 0

    ready = [set() for _ in range(layers)]
    seen = [set() for _ in range(layers)]
    waiting = [[] for _ in range(layers)]

    def activate(l, group, x, start):
        lo, hi = (band(c) for c in columns(group, halos[l], 2**l))
        size = x.shape[0]
        for a, begin, end in ((-1, 0, edge), (0, edge, edge + tile), (1, edge + tile, rows)):
            begin, end = max(begin, start), min(end, start + size)
            if begin < end:
                g = gelu(x[begin - start : end - start].astype(jnp.bfloat16)).astype(jnp.float32)
                if (a, lo, hi) != (0, 0, 0):
                    g = g * pick(keeps[a, lo], keeps[a, hi])
                g_ref[group, BASE + begin : BASE + end, :] = g

    def mirror(l, group):
        halo, dil = halos[l], 2**l
        deep = -(-halo // 8) * 8
        cols = columns(group, halo, dil)
        seen[l].update(cols)
        if any(tile <= c < tile + halo for c in cols):
            for c, value in zip(cols, both(g_ref[group, top:bot, :])):
                if c >= tile:
                    side_ref[pl.ds(c - tile, edge + tile, stride=side_step), :] = value
        if any(0 <= c < tile for c in cols):
            for c, value in zip(cols, both(g_ref[group, top:mid, :])):
                if 0 <= c < tile:
                    left_ref[pl.ds(c, edge, stride=left_step), :] = value
        if any(0 <= c < halo for c in cols):
            for c, value in zip(cols, both(g_ref[group, bot - edge : bot, :])):
                if 0 <= c < halo:
                    corner_ref[pl.ds(c, edge, stride=side_step), :] = value
        waiting[l].append(group)
        for group in list(waiting[l]):
            c1, c2 = columns(group, halo, dil)
            if c1 < tile and not seen[l].issuperset(range(tile, tile + halo)):
                continue
            if c1 < 0 and not seen[l].issuperset(range(tile)):
                continue
            waiting[l].remove(group)
            ready[l].add(group)
            if c1 < tile:
                now = g_ref[group, bot : bot + deep, :]
                at = [(c + edge) * side_step for c in (c1, c2)]
                made = [side_ref[k : k + deep, :] if c < tile else now for c, k in zip((c1, c2), at)]
                new = jnp.where(diagonal, pick(*made), now)
                if c1 < 0:
                    made = [corner_ref[k : k + deep, :] if c < 0 else now for c, k in zip((c1, c2), at)]
                    new = jnp.where(beside, pick(*made), new)
                g_ref[group, bot : bot + deep, :] = new
            if c1 < 0:
                now = g_ref[group, mid:bot, :]
                at = [(c + edge) * left_step for c in (c1, c2)]
                made = [left_ref[k : k + tile, :] if c < 0 else now for c, k in zip((c1, c2), at)]
                g_ref[group, mid:bot, :] = jnp.where(diagonal, pick(*made), now)

    def begin(group):
        x = row_bins + col_bins[group : group + 1]
        x_ref[0, group, :, :] = x
        activate(0, group, x, 0)
        ready[0].add(group)

    stretch = 2**layers
    runs = stretch // 2 // GROUP

    def sends(j, run):
        copies = []
        for k in range(4):
            first = 2 * stretch * j + run * GROUP + k * stretch // 2
            here = (slice(None), pl.ds(first * ch, GROUP * ch))
            copies.append(
                pltpu.make_async_copy(made_ref.at[here], out_ref.at[here], sems.at[(j * runs + run) * 4 + k])
            )
        return copies

    def finish(l, some, acc):
        dil = 2**l
        start = (edge - halos[l + 1]) // 8 * 8
        size = rows - 2 * start
        for n, (j, e) in enumerate(some):
            old = [x_ref[l % 2, (2 * j + s) * dil + e, start : start + size, :] for s in range(3)]
            carried = (pick(pltpu.roll(old[0], ch, 1), old[1]), pick(old[1], pltpu.roll(old[2], ch, 1)))
            new = [
                acc[n * size : (n + 1) * size, s * wide : (s + 1) * wide] + carried[s] + cb_ref[l : l + 1, :]
                for s in range(2)
            ]
            if l + 1 < layers:
                for s, x in enumerate(new):
                    group = j * 2 * dil + e + s * dil
                    x_ref[(l + 1) % 2, group, start : start + size, :] = x
                    activate(l + 1, group, x, start)
                    mirror(l + 1, group)
            elif e % 2 == 0:
                even = new
            else:
                for s in range(2):
                    col = (stretch * 2 * j + e - 1 + s * dil) * ch
                    value = pick(even[s], pltpu.roll(new[s], ch, 1))
                    made_ref[:, col : col + wide] = value.astype(made_ref.dtype)
                    col += stretch * ch
                    value = pick(pltpu.roll(even[s], ch, 1), new[s])
                    made_ref[:, col : col + wide] = value.astype(made_ref.dtype)
                if e % GROUP == GROUP - 1:
                    for copy in sends(j, e // GROUP):
                        copy.start()

    unfinished = None
    for l in range(layers):
        dil = 2**l
        start = (edge - halos[l + 1]) // 8 * 8
        size = rows - 2 * start
        count = (tile + 2 * halos[l + 1]) // (4 * dil)
        blocks = [(j, e) for j in reversed(range(count)) for e in range(dil)]
        group_size = GROUP if l else FIRST_GROUP
        for at in range(0, len(blocks), group_size):
            some = blocks[at : at + group_size]
            need = [(2 * j + s) * dil + e for j, e in some for s in range(3)]
            if l == 0:
                for group in need:
                    if group not in ready[0]:
                        begin(group)
            if not ready[l].issuperset(need):
                finish(*unfinished)
                unfinished = None
            assert ready[l].issuperset(need)

            def taps(j, e):
                return [
                    g_ref[(2 * j + s) * dil + e, BASE + start + i * dil : BASE + start + i * dil + size, :].astype(
                        jnp.bfloat16
                    )
                    for i in (-1, 0, 1)
                    for s in range(3)
                ]

            lhs = jnp.concatenate([jnp.concatenate(taps(j, e), axis=1) for j, e in some], axis=0)
            acc = jnp.dot(lhs, t_refs[l][...], preferred_element_type=jnp.float32)
            if unfinished:
                finish(*unfinished)
            unfinished = (l, some, acc)
    finish(*unfinished)
    for j in range(tile // (2 * stretch)):
        for run in range(runs):
            for copy in sends(j, run):
                copy.wait()


def tile_call(npos, noff, order, layers, block_slot, table, proj_bias, conv_bias, banded):
    tile = 2 * table.shape[1]
    ch = proj_bias.shape[1] // 2
    vmem = pl.BlockSpec(memory_space=pltpu.VMEM)
    wide = 2 * ch
    groups = tile // 2 + 2**layers - 1
    high = tile + 2 * EDGE
    return pl.pallas_call(
        functools.partial(tile_kernel, (layers, tile, ch, npos, noff, order)),
        out_shape=jax.ShapeDtypeStruct((tile, tile * ch), jnp.bfloat16),
        in_specs=[pl.BlockSpec(memory_space=pltpu.SMEM)]
        + [vmem] * (3 + layers),
        out_specs=pl.BlockSpec(memory_space=pl.ANY),
        scratch_shapes=[
            pltpu.VMEM((2, groups, high, wide), jnp.float32),
            pltpu.VMEM((groups, high + 2 * BASE, wide), jnp.float32),
            pltpu.VMEM(((EDGE + 1) * (EDGE + tile), wide), jnp.float32),
            pltpu.VMEM(((tile + 1) * EDGE, wide), jnp.float32),
            pltpu.VMEM(((EDGE + 1) * EDGE, wide), jnp.float32),
            pltpu.VMEM((high, wide), jnp.float32),
            pltpu.VMEM((tile, tile * ch), jnp.bfloat16),
            pltpu.SemaphoreType.DMA((tile // GROUP,)),
        ],
        compiler_params=pltpu.CompilerParams(vmem_limit_bytes=48 * 1024 * 1024),
        cost_estimate=pl.CostEstimate(flops=8000000000, bytes_accessed=4000000, transcendentals=2000000),
    )(block_slot, table, proj_bias, conv_bias, *banded)


def project(emb, weight):
    made = lax.dot_general(emb, weight, (((1,), (1,)), ((), ())), preferred_element_type=jnp.float32)
    half = made.shape[0] // 2
    return jnp.concatenate([made[:half], made[half:]], axis=1).astype(jnp.bfloat16)


def parameters_kernel(
    slot_ref, emb_ref, pw_ref, pb_ref, cb_ref, cw_ref, slot2_ref, own_ref, pw2_ref, pb2_ref, cb2_ref, cw2_ref
):
    for b in range(slot_ref.shape[0]):
        slot2_ref[b] = slot_ref[b]
    own_ref[0] = project(emb_ref[...], pw_ref[...])
    pw2_ref[...] = pw_ref[...]
    cw2_ref[...] = cw_ref[...]
    for ref, to in ((pb_ref, pb2_ref), (cb_ref, cb2_ref)):
        to[...] = jnp.concatenate([ref[...]] * 2, axis=1)


def parameters_call(block_slot, bin_embed, proj_weight, proj_bias, conv_bias, weights):
    vmem, smem = pl.BlockSpec(memory_space=pltpu.VMEM), pl.BlockSpec(memory_space=pltpu.SMEM)
    tile, ch = bin_embed.shape[0], proj_weight.shape[0]
    return pl.pallas_call(
        parameters_kernel,
        out_shape=(
            pltpu.SMEM(block_slot.shape, block_slot.dtype),
            pltpu.VMEM((1, tile // 2, 2 * ch), jnp.bfloat16),
            pltpu.VMEM(proj_weight.shape, proj_weight.dtype),
            pltpu.VMEM((1, 2 * ch), proj_bias.dtype),
            pltpu.VMEM((conv_bias.shape[0], 2 * ch), conv_bias.dtype),
            pltpu.VMEM(weights.shape, weights.dtype),
        ),
        in_specs=[smem] + [vmem] * 5,
        out_specs=(smem,) + (vmem,) * 5,
        cost_estimate=pl.CostEstimate(flops=1000000, bytes_accessed=1000000, transcendentals=0),
    )(block_slot, bin_embed, proj_weight, proj_bias, conv_bias, weights)


def project_kernel(own_ref, emb_ref, pw_ref, out_ref):
    count = emb_ref.shape[0]
    if own_ref is not None:
        out_ref[0] = own_ref[0]
    for b in range(count):
        out_ref[out_ref.shape[0] - count + b] = project(emb_ref[b], pw_ref[...])


def project_call(own, embeds, proj_weight):
    vmem = pl.BlockSpec(memory_space=pltpu.VMEM)
    blocks, tile, _ = embeds.shape
    ch = proj_weight.shape[0]
    kernel, args = project_kernel, (own, embeds, proj_weight)
    if own is None:
        kernel, args = functools.partial(project_kernel, None), args[1:]
    args = [pltpu.with_memory_space_constraint(arg, pltpu.VMEM) for arg in args]
    return pl.pallas_call(
        kernel,
        out_shape=pltpu.VMEM((blocks + len(args) - 2, tile // 2, 2 * ch), jnp.bfloat16),
        in_specs=[vmem] * len(args),
        out_specs=vmem,
        cost_estimate=pl.CostEstimate(flops=1000000, bytes_accessed=100000, transcendentals=0),
    )(*args)


def band_call(weights, which):
    layers, ch, taps = weights.shape
    weights = pltpu.with_memory_space_constraint(weights, pltpu.VMEM)
    vmem = pl.BlockSpec(memory_space=pltpu.VMEM)
    return pl.pallas_call(
        functools.partial(weights_kernel, ch, which),
        out_shape=(pltpu.VMEM((2 * taps, 4 * ch), weights.dtype),) * len(which),
        in_specs=[vmem],
        out_specs=(vmem,) * len(which),
        cost_estimate=pl.CostEstimate(flops=1000000, bytes_accessed=1000000, transcendentals=0),
    )(weights)


def on_device(bin_embed, block_slot, proj_weight, proj_bias, conv_weight, conv_bias):
    npos, noff = lax.axis_size("pos"), lax.axis_size("off")
    tile, emb = bin_embed.shape
    layers, taps, ch = conv_weight.shape
    order = tuple(reversed(range(npos.bit_length() - 1))) if npos & (npos - 1) == 0 else ()
    turned = jnp.swapaxes(conv_weight, 1, 2)
    table = bin_embed[None]
    banded, todo = [], tuple(range(layers))
    small = (block_slot, bin_embed, proj_weight.T, proj_bias[None], conv_bias, turned)
    for stage, bit in enumerate(order):
        there = lax.ppermute(table, "pos", [(i, i ^ (1 << bit | 1)) for i in range(npos)])
        if stage == 0:
            slots, table, projection, *small, turned = parameters_call(*small)
            there, table, small, slots, turned = lax.optimization_barrier((there, table, small, slots, turned))
            table = project_call(table, there, projection)
            continue
        if todo:
            made = band_call(turned, todo[:2])
            there, made, turned = lax.optimization_barrier((there, made, turned))
            banded, todo = banded + list(made), todo[2:]
        table = jnp.concatenate([table, there], axis=0)
    if not order:
        slots, _, projection, *small, turned = parameters_call(*small)
        table = project_call(None, lax.all_gather(bin_embed, "pos"), projection)
    if todo:
        banded += band_call(turned, todo)
    out = tile_call(npos, noff, order, layers, slots, table, *small, banded)
    return out.reshape(1, 1, tile, tile * ch)


def solution(mesh):
    placed = (P("pos", None), P(), P(), P(), P(), P())
    return jax.shard_map(
        on_device,
        mesh=mesh,
        in_specs=placed,
        out_specs=P("pos", "off", None, None),
        check_vma=False,
    )
```

```python
import functools

import jax
import jax.numpy as jnp
from jax import lax
from jax.experimental import pallas as pl
from jax.experimental.pallas import tpu as pltpu
from jax.sharding import PartitionSpec as P

GROUP = 4
FIRST_GROUP = 6
BASE = 8
EDGE = 16


def gelu(x):
    u = x * (0.7978845608028654 + 0.035677408136300125 * (x * x))
    half = 0.5 * x
    return half + half * jnp.tanh(u)


def place(col, halo, dil):
    u = col + halo
    within = u % (2 * dil)
    return (u // (2 * dil)) * dil + within % dil, within // dil


def columns(group, halo, dil):
    first = (group // dil) * 2 * dil + group % dil - halo
    return first, first + dil


def weights_kernel(ch, which, cw_ref, *t_refs):
    zero = jnp.zeros((ch, ch), cw_ref.dtype)
    for l, t_ref in zip(which, t_refs):
        taps = jnp.transpose(cw_ref[l].astype(jnp.float32)).astype(t_ref.dtype)
        for i in range(3):
            for a in range(6):
                row = [
                    taps[(3 * i + a - b) * ch : (3 * i + a - b + 1) * ch] if 0 <= a - b <= 2 else zero
                    for b in (0, 2, 1, 3)
                ]
                t_ref[(6 * i + a) * ch : (6 * i + a + 1) * ch, :] = jnp.concatenate(row, axis=1)


def tile_kernel(dims, slot_ref, bin_ref, pb_ref, cb_ref, *refs):
    layers, tile, ch, npos, noff, order = dims
    t_refs = refs[:layers]
    out_ref, x_ref, g_ref, side_ref, left_ref, corner_ref, bins_ref, made_ref, sems = refs[layers:]
    wide = 2 * ch
    edge = EDGE
    rows = tile + 2 * edge
    halos = [2**layers - 2**l for l in range(layers + 1)]
    top, mid, bot = BASE, BASE + edge, BASE + edge + tile
    side_step, left_step = edge + 1, tile + 1
    me, off = lax.axis_index("pos"), lax.axis_index("off")
    low = lax.broadcasted_iota(jnp.int32, (1, wide), 1) < ch
    diagonal, beside = off == 0, off == 1

    def pick(lo, hi):
        return jnp.where(low, lo, hi)

    def both(value):
        turned = pltpu.roll(value, ch, 1)
        return pick(value, turned), pick(turned, value)

    def block(b):
        slot = slot_ref[lax.rem(b + npos, npos)]
        if not order:
            return slot
        away = jnp.bitwise_xor(slot, me)
        bits = [jnp.bitwise_and(lax.shift_right_logical(away, bit), 1) for bit in order]
        for bit in bits[:-1]:
            bits[-1] = jnp.bitwise_xor(bits[-1], bit)
        return sum(bit << n for n, bit in enumerate(bits))

    def bins(b):
        first, here, last = (both(bin_ref[block(b + k)].astype(jnp.float32)) for k in (-1, 0, 1))
        return jnp.concatenate([first[1][tile // 2 - edge :], here[0], here[1], last[0][:edge]], axis=0)

    row_bins = bins(me) + pb_ref[...]
    bins_ref[...] = bins(me + off)
    pairs = (tile + 2 * halos[0]) // 2
    first = edge - halos[0]
    col_bins = pick(
        bins_ref[pl.ds(first, pairs, stride=2), :], bins_ref[pl.ds(first + 1, pairs, stride=2), :]
    )

    keeps = {
        (a, b): (jnp.abs(off + b - a) < noff).astype(jnp.float32) for a in (-1, 0, 1) for b in (-1, 0, 1)
    }

    def band(col):
        return -1 if col < 0 else 1 if col >= tile else 0

    ready = [set() for _ in range(layers)]
    seen = [set() for _ in range(layers)]
    waiting = [[] for _ in range(layers)]

    def activate(l, group, x, start):
        lo, hi = (band(c) for c in columns(group, halos[l], 2**l))
        size = x.shape[0]
        for a, begin, end in ((-1, 0, edge), (0, edge, edge + tile), (1, edge + tile, rows)):
            begin, end = max(begin, start), min(end, start + size)
            if begin < end:
                g = gelu(x[begin - start : end - start].astype(jnp.bfloat16)).astype(jnp.float32)
                if (a, lo, hi) != (0, 0, 0):
                    g = g * pick(keeps[a, lo], keeps[a, hi])
                g_ref[group, BASE + begin : BASE + end, :] = g

    def mirror(l, group):
        halo, dil = halos[l], 2**l
        deep = -(-halo // 8) * 8
        cols = columns(group, halo, dil)
        seen[l].update(cols)
        if any(tile <= c < tile + halo for c in cols):
            for c, value in zip(cols, both(g_ref[group, top:bot, :])):
                if c >= tile:
                    side_ref[pl.ds(c - tile, edge + tile, stride=side_step), :] = value
        if any(0 <= c < tile for c in cols):
            for c, value in zip(cols, both(g_ref[group, top:mid, :])):
                if 0 <= c < tile:
                    left_ref[pl.ds(c, edge, stride=left_step), :] = value
        if any(0 <= c < halo for c in cols):
            for c, value in zip(cols, both(g_ref[group, bot - edge : bot, :])):
                if 0 <= c < halo:
                    corner_ref[pl.ds(c, edge, stride=side_step), :] = value
        waiting[l].append(group)
        for group in list(waiting[l]):
            c1, c2 = columns(group, halo, dil)
            if c1 < tile and not seen[l].issuperset(range(tile, tile + halo)):
                continue
            if c1 < 0 and not seen[l].issuperset(range(tile)):
                continue
            waiting[l].remove(group)
            ready[l].add(group)
            if c1 < tile:
                now = g_ref[group, bot : bot + deep, :]
                at = [(c + edge) * side_step for c in (c1, c2)]
                made = [side_ref[k : k + deep, :] if c < tile else now for c, k in zip((c1, c2), at)]
                new = jnp.where(diagonal, pick(*made), now)
                if c1 < 0:
                    made = [corner_ref[k : k + deep, :] if c < 0 else now for c, k in zip((c1, c2), at)]
                    new = jnp.where(beside, pick(*made), new)
                g_ref[group, bot : bot + deep, :] = new
            if c1 < 0:
                now = g_ref[group, mid:bot, :]
                at = [(c + edge) * left_step for c in (c1, c2)]
                made = [left_ref[k : k + tile, :] if c < 0 else now for c, k in zip((c1, c2), at)]
                g_ref[group, mid:bot, :] = jnp.where(diagonal, pick(*made), now)

    def begin(group):
        x = row_bins + col_bins[group : group + 1]
        x_ref[0, group, :, :] = x
        activate(0, group, x, 0)
        ready[0].add(group)

    stretch = 2**layers
    span = 2 * stretch * ch

    def send(j):
        here = (slice(None), pl.ds(j * span, span))
        return pltpu.make_async_copy(made_ref.at[here], out_ref.at[here], sems.at[j])

    def finish(l, some, acc):
        dil = 2**l
        start = (edge - halos[l + 1]) // 8 * 8
        size = rows - 2 * start
        for n, (j, e) in enumerate(some):
            old = [x_ref[l % 2, (2 * j + s) * dil + e, start : start + size, :] for s in range(3)]
            carried = (pick(pltpu.roll(old[0], ch, 1), old[1]), pick(old[1], pltpu.roll(old[2], ch, 1)))
            new = [
                acc[n * size : (n + 1) * size, s * wide : (s + 1) * wide] + carried[s] + cb_ref[l : l + 1, :]
                for s in range(2)
            ]
            if l + 1 < layers:
                for s, x in enumerate(new):
                    group = j * 2 * dil + e + s * dil
                    x_ref[(l + 1) % 2, group, start : start + size, :] = x
                    activate(l + 1, group, x, start)
                    mirror(l + 1, group)
            elif e % 2 == 0:
                even = new
            else:
                for s in range(2):
                    col = (stretch * 2 * j + e - 1 + s * dil) * ch
                    value = pick(even[s], pltpu.roll(new[s], ch, 1))
                    made_ref[:, col : col + wide] = value.astype(made_ref.dtype)
                    col += stretch * ch
                    value = pick(pltpu.roll(even[s], ch, 1), new[s])
                    made_ref[:, col : col + wide] = value.astype(made_ref.dtype)
                if e == dil - 1:
                    send(j).start()

    unfinished = None
    for l in range(layers):
        dil = 2**l
        start = (edge - halos[l + 1]) // 8 * 8
        size = rows - 2 * start
        count = (tile + 2 * halos[l + 1]) // (4 * dil)
        blocks = [(j, e) for j in reversed(range(count)) for e in range(dil)]
        group_size = GROUP if l else FIRST_GROUP
        for at in range(0, len(blocks), group_size):
            some = blocks[at : at + group_size]
            need = [(2 * j + s) * dil + e for j, e in some for s in range(3)]
            if l == 0:
                for group in need:
                    if group not in ready[0]:
                        begin(group)
            if not ready[l].issuperset(need):
                finish(*unfinished)
                unfinished = None
            assert ready[l].issuperset(need)

            def taps(j, e):
                return [
                    g_ref[(2 * j + s) * dil + e, BASE + start + i * dil : BASE + start + i * dil + size, :].astype(
                        jnp.bfloat16
                    )
                    for i in (-1, 0, 1)
                    for s in range(3)
                ]

            lhs = jnp.concatenate([jnp.concatenate(taps(j, e), axis=1) for j, e in some], axis=0)
            acc = jnp.dot(lhs, t_refs[l][...], preferred_element_type=jnp.float32)
            if unfinished:
                finish(*unfinished)
            unfinished = (l, some, acc)
    finish(*unfinished)
    for j in range(tile // (2 * stretch)):
        send(j).wait()


def tile_call(npos, noff, order, layers, block_slot, table, proj_bias, conv_bias, banded):
    tile = 2 * table.shape[1]
    ch = proj_bias.shape[1] // 2
    vmem = pl.BlockSpec(memory_space=pltpu.VMEM)
    wide = 2 * ch
    groups = tile // 2 + 2**layers - 1
    high = tile + 2 * EDGE
    return pl.pallas_call(
        functools.partial(tile_kernel, (layers, tile, ch, npos, noff, order)),
        out_shape=jax.ShapeDtypeStruct((tile, tile * ch), jnp.bfloat16),
        in_specs=[pl.BlockSpec(memory_space=pltpu.SMEM)]
        + [vmem] * (3 + layers),
        out_specs=pl.BlockSpec(memory_space=pl.ANY),
        scratch_shapes=[
            pltpu.VMEM((2, groups, high, wide), jnp.float32),
            pltpu.VMEM((groups, high + 2 * BASE, wide), jnp.float32),
            pltpu.VMEM(((EDGE + 1) * (EDGE + tile), wide), jnp.float32),
            pltpu.VMEM(((tile + 1) * EDGE, wide), jnp.float32),
            pltpu.VMEM(((EDGE + 1) * EDGE, wide), jnp.float32),
            pltpu.VMEM((high, wide), jnp.float32),
            pltpu.VMEM((tile, tile * ch), jnp.bfloat16),
            pltpu.SemaphoreType.DMA((tile // 2 ** (layers + 1),)),
        ],
        compiler_params=pltpu.CompilerParams(vmem_limit_bytes=20 * 1024 * 1024),
        cost_estimate=pl.CostEstimate(flops=8000000000, bytes_accessed=4000000, transcendentals=2000000),
    )(block_slot, table, proj_bias, conv_bias, *banded)


def project(emb, weight):
    made = lax.dot_general(emb, weight, (((1,), (1,)), ((), ())), preferred_element_type=jnp.float32)
    half = made.shape[0] // 2
    return jnp.concatenate([made[:half], made[half:]], axis=1).astype(jnp.bfloat16)


def parameters_kernel(
    slot_ref, emb_ref, pw_ref, pb_ref, cb_ref, cw_ref, slot2_ref, own_ref, pw2_ref, pb2_ref, cb2_ref, cw2_ref
):
    for b in range(slot_ref.shape[0]):
        slot2_ref[b] = slot_ref[b]
    own_ref[0] = project(emb_ref[...], pw_ref[...])
    pw2_ref[...] = pw_ref[...]
    cw2_ref[...] = cw_ref[...]
    for ref, to in ((pb_ref, pb2_ref), (cb_ref, cb2_ref)):
        to[...] = jnp.concatenate([ref[...]] * 2, axis=1)


def parameters_call(block_slot, bin_embed, proj_weight, proj_bias, conv_bias, weights):
    vmem, smem = pl.BlockSpec(memory_space=pltpu.VMEM), pl.BlockSpec(memory_space=pltpu.SMEM)
    tile, ch = bin_embed.shape[0], proj_weight.shape[0]
    return pl.pallas_call(
        parameters_kernel,
        out_shape=(
            pltpu.SMEM(block_slot.shape, block_slot.dtype),
            pltpu.VMEM((1, tile // 2, 2 * ch), jnp.bfloat16),
            pltpu.VMEM(proj_weight.shape, proj_weight.dtype),
            pltpu.VMEM((1, 2 * ch), proj_bias.dtype),
            pltpu.VMEM((conv_bias.shape[0], 2 * ch), conv_bias.dtype),
            pltpu.VMEM(weights.shape, weights.dtype),
        ),
        in_specs=[smem] + [vmem] * 5,
        out_specs=(smem,) + (vmem,) * 5,
        cost_estimate=pl.CostEstimate(flops=1000000, bytes_accessed=1000000, transcendentals=0),
    )(block_slot, bin_embed, proj_weight, proj_bias, conv_bias, weights)


def project_kernel(own_ref, emb_ref, pw_ref, out_ref):
    count = emb_ref.shape[0]
    if own_ref is not None:
        out_ref[0] = own_ref[0]
    for b in range(count):
        out_ref[out_ref.shape[0] - count + b] = project(emb_ref[b], pw_ref[...])


def project_call(own, embeds, proj_weight):
    vmem = pl.BlockSpec(memory_space=pltpu.VMEM)
    blocks, tile, _ = embeds.shape
    ch = proj_weight.shape[0]
    kernel, args = project_kernel, (own, embeds, proj_weight)
    if own is None:
        kernel, args = functools.partial(project_kernel, None), args[1:]
    args = [pltpu.with_memory_space_constraint(arg, pltpu.VMEM) for arg in args]
    return pl.pallas_call(
        kernel,
        out_shape=pltpu.VMEM((blocks + len(args) - 2, tile // 2, 2 * ch), jnp.bfloat16),
        in_specs=[vmem] * len(args),
        out_specs=vmem,
        cost_estimate=pl.CostEstimate(flops=1000000, bytes_accessed=100000, transcendentals=0),
    )(*args)


def band_call(weights, which):
    layers, ch, taps = weights.shape
    weights = pltpu.with_memory_space_constraint(weights, pltpu.VMEM)
    vmem = pl.BlockSpec(memory_space=pltpu.VMEM)
    return pl.pallas_call(
        functools.partial(weights_kernel, ch, which),
        out_shape=(pltpu.VMEM((2 * taps, 4 * ch), weights.dtype),) * len(which),
        in_specs=[vmem],
        out_specs=(vmem,) * len(which),
        cost_estimate=pl.CostEstimate(flops=1000000, bytes_accessed=1000000, transcendentals=0),
    )(weights)


def on_device(bin_embed, block_slot, proj_weight, proj_bias, conv_weight, conv_bias):
    npos, noff = lax.axis_size("pos"), lax.axis_size("off")
    tile, emb = bin_embed.shape
    layers, taps, ch = conv_weight.shape
    order = tuple(reversed(range(npos.bit_length() - 1))) if npos & (npos - 1) == 0 else ()
    turned = jnp.swapaxes(conv_weight, 1, 2)
    table = bin_embed[None]
    banded, todo = [], tuple(range(layers))
    small = (block_slot, bin_embed, proj_weight.T, proj_bias[None], conv_bias, turned)
    for stage, bit in enumerate(order):
        there = lax.ppermute(table, "pos", [(i, i ^ (1 << bit | 1)) for i in range(npos)])
        if stage == 0:
            slots, table, projection, *small, turned = parameters_call(*small)
            there, table, small, slots, turned = lax.optimization_barrier((there, table, small, slots, turned))
            table = project_call(table, there, projection)
            continue
        if todo:
            made = band_call(turned, todo[:2])
            there, made, turned = lax.optimization_barrier((there, made, turned))
            banded, todo = banded + list(made), todo[2:]
        table = jnp.concatenate([table, there], axis=0)
    if not order:
        slots, _, projection, *small, turned = parameters_call(*small)
        table = project_call(None, lax.all_gather(bin_embed, "pos"), projection)
    if todo:
        banded += band_call(turned, todo)
    out = tile_call(npos, noff, order, layers, slots, table, *small, banded)
    return out.reshape(1, 1, tile, tile * ch)


def solution(mesh):
    placed = (P("pos", None), P(), P(), P(), P(), P())
    return jax.shard_map(
        on_device,
        mesh=mesh,
        in_specs=placed,
        out_specs=P("pos", "off", None, None),
        check_vma=False,
    )
```
